32 devices in a mesh: group: 4 (over y, x), dom: 8 (over z, core).
Axes of the slice: x: 2, y: 2, z: 4, core: 2. Of those that a mesh axis runs over, the one named last changes fastest.
Arguments:
- feats: bfloat16 [65536, 128], P(('group', 'dom')), may hold values from -6 to 6
- coords: bfloat16 [3, 65536], P(None, ('group', 'dom')), may hold values from 0 to 1
- msg_cot: bfloat16 [65536, 128], P(('group', 'dom')), may hold values from -6 to 6
- send_list: int32 [32, 4, 2], P(('group', 'dom')), may hold values from 0 to 15
- tiles: int32 [32, 96, 2], P(('group', 'dom')), may hold values from 0 to 23, as said below
- tile_count: int32 [32], P(('group', 'dom')), may hold values from 24 to 96, as said below
- wavevec: int32 [512, 3], replicated, may hold values from -4 to 4
- w_rad_a: bfloat16 [128, 128], replicated, may hold values from -0.5 to 0.5
- w_rad_b: bfloat16 [128, 128], replicated, may hold values from -0.5 to 0.5
- w_charge: bfloat16 [128, 128], replicated, may hold values from -0.5 to 0.5
- w_long: bfloat16 [128, 128], replicated, may hold values from -0.5 to 0.5
- norm_gain: float32 [128], replicated, may hold values from 0.1 to 1.9
- w_in: bfloat16 [128, 256], replicated, may hold values from -0.5 to 0.5
- w_out: bfloat16 [256, 128], replicated, may hold values from -0.375 to 0.375
Outputs:
- new_feats: bfloat16 [65536, 128], P(('group', 'dom'))
- feat_adjoint: float32 [65536, 128], P(('group', 'dom'))
The draws below stay inside these ranges and needn't reach their ends.
Inputs may be any that keep to these rules, and one draw needn't show every extreme that they name: In every domain the first 8 tiles have source blocks 16, 17, ... in order, one each; targets are below 16 and sources below 24. `tile_count`: tiles at or after a domain's count are not used; some domain has all 96 live.
All inputs are finite; a program needn't handle non-finite values.
Results may differ from the reference program's by a relative error of at most 0.0067.
Values may be sent and summed in bfloat16 or wider, within the bound.
No kernel may reach another device: no remote copies, remote signals or barrier semaphores. Data moves between devices by JAX's collectives and lax.ppermute only.
A program may use at most 64 MiB of HBM per device.

```python
import jax
import jax.numpy as jnp
from jax import lax

F = 128
QC = 128
HID = 256
K = 512
BLK = 128
HB = 2
ATOMS_DEV = 2048
NBLK = 16
MAXT = 96
ATOMS = 65536
N_GROUP = 4
N_DOM = 8
DEVICES = 32


def draw_tiles(key, part):
    target = jax.random.randint(jax.random.fold_in(key, 11), (DEVICES, MAXT), 0, NBLK)
    source = jax.random.randint(jax.random.fold_in(key, 12), (DEVICES, MAXT), 0, NBLK + 4 * HB)
    ordinal = jnp.arange(MAXT, dtype=jnp.int32)
    source = jnp.where(ordinal[None, :] < 4 * HB, NBLK + ordinal[None, :], source)
    return jnp.stack([target, source], axis=-1).astype(jnp.int32)


def draw_tile_count(key, part):
    lowest = MAXT // 4
    span = MAXT - lowest + 1
    rolled = jax.random.randint(jax.random.fold_in(key, 21), (DEVICES,), 0, span)
    count = lowest + rolled * rolled * rolled // (span * span)
    busiest = jax.random.randint(jax.random.fold_in(key, 22), (), 0, DEVICES)
    count = jnp.where(jnp.arange(DEVICES) == busiest, MAXT, count)
    return count.astype(jnp.int32)


def plant(drawn, key, least, high):
    shape = drawn.shape
    spot = [jax.random.randint(jax.random.fold_in(key, axis), (), 0, shape[axis]) for axis in range(len(shape))]
    drawn = drawn.at[tuple(spot)].set(least)
    longest = shape.index(max(shape))
    spot[longest] = (spot[longest] + 1) % shape[longest]
    return drawn.at[tuple(spot)].set(high)


def shard_levels(own_key, dims, split, least, largest):
    loudness = 1.0
    for position, shards_of in split:
        steps = jax.random.uniform(jax.random.fold_in(jax.random.fold_in(own_key, 6), position), (shards_of,), jnp.float32, least / len(split), largest / len(split))
        loudness = loudness * jnp.repeat(jnp.exp(steps), dims[position] // shards_of).reshape((-1,) + (1,) * (len(dims) - 1 - position))
    return loudness


def bell_draw(stream_key, shape, deviation, bound, pieces=(), kind=jnp.bfloat16):
    array = deviation * jax.random.normal(stream_key, shape, jnp.float32)
    if pieces:
        array = array * shard_levels(stream_key, shape, pieces, -0.22, 0.18)
    return jnp.clip(array, -bound, bound).astype(kind)


def setup_inputs(seed: int = 0) -> dict:
    seeds = jax.random.split(jax.random.key(seed), 15)
    feats = bell_draw(seeds[0], (ATOMS, F), 1.0, 6.0, ((0, 32),))
    coords = jnp.clip(1.0 * jax.random.uniform(seeds[1], (3, ATOMS), jnp.float32) ** shard_levels(seeds[1], (3, ATOMS), ((1, 32),), -0.2, 0.2), 0.0, 1.0).astype(jnp.bfloat16)
    msg_cot = bell_draw(seeds[2], (ATOMS, F), 1.0, 6.0, ((0, 32),))
    send_list = plant(jax.random.randint(seeds[3], (DEVICES, 4, HB), 0, NBLK), jax.random.fold_in(seeds[3], 1), 0, NBLK - 1).astype(jnp.int32)
    tiles = draw_tiles(jax.random.fold_in(seeds[14], 71), 0)
    tile_count = draw_tile_count(jax.random.fold_in(seeds[14], 71), 0)
    wavevec = plant(jax.random.randint(seeds[6], (K, 3), -4, 5), jax.random.fold_in(seeds[6], 1), -4, 4).astype(jnp.int32)
    w_rad_a = bell_draw(seeds[7], (F, F), F ** -0.5, 0.5)
    w_rad_b = bell_draw(seeds[8], (F, F), F ** -0.5, 0.5)
    w_charge = bell_draw(seeds[9], (F, QC), F ** -0.5, 0.5)
    w_long = bell_draw(seeds[10], (QC, F), QC ** -0.5, 0.5)
    norm_gain = jnp.clip(1.0 + 0.18 * jax.random.normal(seeds[11], (F,), jnp.float32), 0.1, 1.9)
    w_in = bell_draw(seeds[12], (F, HID), F ** -0.5, 0.5)
    w_out = bell_draw(seeds[13], (HID, F), HID ** -0.5, 0.375)
    return {"feats": feats, "coords": coords, "msg_cot": msg_cot, "send_list": send_list, "tiles": tiles, "tile_count": tile_count, "wavevec": wavevec, "w_rad_a": w_rad_a, "w_rad_b": w_rad_b, "w_charge": w_charge, "w_long": w_long, "norm_gain": norm_gain, "w_in": w_in, "w_out": w_out}


RADIAL_A = 6.0
RADIAL_B = 30.0
MSG_SCALE = 1.0 / 32.0

def tile_pass(ext_feats, ext_xyz, cot_blocks, tiles_dev, count, w_rad_a, w_rad_b):
    extent = ext_feats.shape[0]
    flat = ext_feats.reshape(extent * BLK, F)
    proj_a = jnp.dot(flat, w_rad_a, preferred_element_type=jnp.float32).astype(jnp.bfloat16).reshape(extent, BLK, F)
    proj_b = jnp.dot(flat, w_rad_b, preferred_element_type=jnp.float32).astype(jnp.bfloat16).reshape(extent, BLK, F)

    def one_tile(step, carry):
        msg, grad_a, grad_b = carry
        target = tiles_dev[step, 0]
        source = tiles_dev[step, 1]
        live = jnp.where(step < count, jnp.float32(1.0), jnp.float32(0.0))
        diff = ext_xyz[:, target][:, :, None] - ext_xyz[:, source][:, None, :]
        dist2 = lax.optimization_barrier(jnp.sum(diff * diff, axis=0))
        ker_a = jnp.exp(-RADIAL_A * dist2).astype(jnp.bfloat16)
        ker_b = jnp.exp(-RADIAL_B * dist2).astype(jnp.bfloat16)
        term = jnp.dot(ker_a, proj_a[source], preferred_element_type=jnp.float32)
        term = term + jnp.dot(ker_b, proj_b[source], preferred_element_type=jnp.float32)
        msg = msg.at[target].add(live * term)
        back_a = jnp.dot(ker_a.T, cot_blocks[target], preferred_element_type=jnp.float32)
        back_b = jnp.dot(ker_b.T, cot_blocks[target], preferred_element_type=jnp.float32)
        grad_a = grad_a.at[source].add(live * back_a)
        grad_b = grad_b.at[source].add(live * back_b)
        return (msg, grad_a, grad_b)
    start = (jnp.zeros((NBLK, BLK, F), jnp.float32), jnp.zeros((extent, BLK, F), jnp.float32), jnp.zeros((extent, BLK, F), jnp.float32))
    msg, grad_a, grad_b = lax.fori_loop(0, MAXT, one_tile, start)
    msg = MSG_SCALE * msg
    grad_a = (MSG_SCALE * grad_a).astype(jnp.bfloat16).reshape(extent * BLK, F)
    grad_b = (MSG_SCALE * grad_b).astype(jnp.bfloat16).reshape(extent * BLK, F)
    grad_ext = jnp.dot(grad_a, w_rad_a.T, preferred_element_type=jnp.float32) + jnp.dot(grad_b, w_rad_b.T, preferred_element_type=jnp.float32)
    return (msg, grad_ext.reshape(extent, BLK, F))

def arrive(sent):
    return jnp.stack([jnp.roll(sent[:, :, 0], 1, axis=1), jnp.roll(sent[:, :, 1], -1, axis=1), jnp.roll(sent[:, :, 2], 1, axis=0), jnp.roll(sent[:, :, 3], -1, axis=0)], axis=2)

def depart(held):
    return jnp.stack([jnp.roll(held[:, :, 0], -1, axis=1), jnp.roll(held[:, :, 1], 1, axis=1), jnp.roll(held[:, :, 2], -1, axis=0), jnp.roll(held[:, :, 3], 1, axis=0)], axis=2)

def reference(feats, coords, msg_cot, send_list, tiles, tile_count, wavevec, w_rad_a, w_rad_b, w_charge, w_long, norm_gain, w_in, w_out):
    blocks = feats.reshape(N_GROUP, N_DOM, NBLK, BLK, F)
    xyz = jnp.moveaxis(coords.reshape(3, N_GROUP, N_DOM, NBLK, BLK), 0, 3)
    lists = send_list.reshape(N_GROUP, N_DOM, 4, HB)
    picked = jax.vmap(jax.vmap(lambda b, l: b[l]))(blocks, lists)
    picked_xyz = jax.vmap(jax.vmap(lambda b, l: b[l]))(xyz, lists)
    ext_feats = jnp.concatenate([blocks, arrive(picked).reshape(N_GROUP, N_DOM, 4 * HB, BLK, F)], axis=2)
    ext_xyz = jnp.concatenate([xyz, arrive(picked_xyz).reshape(N_GROUP, N_DOM, 4 * HB, 3, BLK)], axis=2)
    extent = NBLK + 4 * HB
    ext_feats = ext_feats.reshape(DEVICES, extent, BLK, F)
    ext_xyz = jnp.moveaxis(ext_xyz.reshape(DEVICES, extent, 3, BLK), 2, 1).astype(jnp.float32)
    cot_blocks = msg_cot.reshape(DEVICES, NBLK, BLK, F)

    def per_domain(items):
        return tile_pass(items[0], items[1], items[2], items[3], items[4], w_rad_a, w_rad_b)
    msg, grad_ext = lax.map(per_domain, (ext_feats, ext_xyz, cot_blocks, tiles, tile_count))
    grad_ext = grad_ext.reshape(N_GROUP, N_DOM, extent, BLK, F)
    held = grad_ext[:, :, NBLK:].reshape(N_GROUP, N_DOM, 4, HB, BLK, F)
    returned = depart(held).reshape(N_GROUP, N_DOM, 4 * HB, BLK, F)
    place = jax.nn.one_hot(lists.reshape(N_GROUP, N_DOM, 4 * HB), NBLK, dtype=jnp.float32)
    adjoint = grad_ext[:, :, :NBLK] + jnp.einsum('gdhb,gdhif->gdbif', place, returned, precision=lax.Precision.HIGHEST)
    feat_adjoint = adjoint.reshape(ATOMS, F)
    wave = wavevec.astype(jnp.float32)
    norm2 = lax.optimization_barrier(jnp.sum(wave * wave, axis=1))
    strength = jnp.exp(-norm2 / 16.0) / (1.0 + norm2) * float(ATOMS_DEV * N_DOM) ** (-0.5)
    group_atoms = N_DOM * ATOMS_DEV
    frac_groups = jnp.moveaxis(coords.astype(jnp.float32).reshape(3, N_GROUP, group_atoms), 1, 0)
    feat_groups = feats.reshape(N_GROUP, group_atoms, F)

    def per_group(items):
        frac, gfeats = items
        phase = 2.0 * jnp.pi * (frac[0][:, None] * wave[:, 0][None, :] + frac[1][:, None] * wave[:, 1][None, :] + frac[2][:, None] * wave[:, 2][None, :])
        cos_t = jnp.cos(phase).astype(jnp.bfloat16)
        sin_t = jnp.sin(phase).astype(jnp.bfloat16)
        charges = jnp.dot(gfeats, w_charge, preferred_element_type=jnp.float32).astype(jnp.bfloat16)
        struct_cos = jnp.dot(cos_t.T, charges, preferred_element_type=jnp.float32)
        struct_sin = jnp.dot(sin_t.T, charges, preferred_element_type=jnp.float32)
        weight_cos = (strength[:, None] * struct_cos).astype(jnp.bfloat16)
        weight_sin = (strength[:, None] * struct_sin).astype(jnp.bfloat16)
        potential = jnp.dot(cos_t, weight_cos, preferred_element_type=jnp.float32) + jnp.dot(sin_t, weight_sin, preferred_element_type=jnp.float32)
        return jnp.dot(potential.astype(jnp.bfloat16), w_long, preferred_element_type=jnp.float32)
    long_msg = lax.map(per_group, (frac_groups, feat_groups)).reshape(ATOMS, F)
    mixed = feats.astype(jnp.float32) + msg.reshape(ATOMS, F) + long_msg
    scale = lax.rsqrt(lax.optimization_barrier(jnp.mean(mixed * mixed, axis=1, keepdims=True)) + 1e-06)
    normed = (mixed * scale * norm_gain[None, :]).astype(jnp.bfloat16)
    hidden = jax.nn.silu(jnp.dot(normed, w_in, preferred_element_type=jnp.float32)).astype(jnp.bfloat16)
    new_feats = (mixed + jnp.dot(hidden, w_out, preferred_element_type=jnp.float32)).astype(jnp.bfloat16)
    return (new_feats, feat_adjoint)
```

```python
import functools

import jax
import jax.numpy as jnp
import numpy as np
from jax import lax
from jax.experimental import pallas as pl
from jax.experimental.pallas import tpu as pltpu
from jax.sharding import PartitionSpec as P

BLK = 128
HB = 2
WMAX = 4
COORD_ROWS = 16

RADIAL_A = 6.0
MSG_SCALE = 1.0 / 32.0
LOG2E = 1.4426950408889634

NT = (((1,), (1,)), ((), ()))
NN = (((1,), (0,)), ((), ()))

VMEM = pltpu.VMEM
SMEM = pltpu.SMEM
BF16 = jnp.bfloat16
F32 = jnp.float32


def dot(a, b, dims=NN):
    return lax.dot_general(a, b, dims, preferred_element_type=F32)


PAIRS = [(0, b) for b in range(1, WMAX + 1)] + [
    (a, b) for a in range(1, WMAX + 1) for b in range(-WMAX, WMAX + 1)
]
NPAIR = len(PAIRS)
BASE_ROWS = 48
HALF = BASE_ROWS + WMAX * 2 * NPAIR


def base_table():
    rows = np.zeros((BASE_ROWS, COORD_ROWS), np.float32)
    for r, (a, b) in enumerate(PAIRS):
        rows[r, 0], rows[r, 1] = a, b
    for m in range(WMAX + 1):
        rows[NPAIR + m, 2] = m
    return rows


def grid_norm2():
    base = (base_table() ** 2).sum(1)
    parts = [base]
    for m in range(1, WMAX + 1):
        parts += [base[:NPAIR] + m * m] * 2
    return np.concatenate(parts).reshape(HALF, 1).astype(np.float32)


def taylor(first, count):
    coef, out = 1.0, []
    for k in range(1, first + 1):
        coef /= k
    power = first
    for _ in range(count):
        out.append(coef)
        coef = -coef / ((power + 1) * (power + 2))
        power += 2
    return out


SIN_COEF = [c * np.pi ** (2 * i + 1) for i, c in enumerate(taylor(1, 7))]
COS_COEF = [c * np.pi ** (2 * i) for i, c in enumerate(taylor(0, 8))]


def horner(z, coefs):
    acc = jnp.full_like(z, coefs[-1])
    for c in coefs[-2::-1]:
        acc = acc * z + c
    return acc


def cos_sin_turns(turns):
    r = turns - jnp.round(turns)
    z = r * r
    s = r * horner(z, SIN_COEF)
    c = horner(z, COS_COEF)
    return 1.0 - 2.0 * (s * s), 2.0 * (s * c)


def trig_chunk(table, xyz16):
    c, s = cos_sin_turns(dot(table, xyz16))
    cos_parts, sin_parts = [c.astype(BF16)], [s.astype(BF16)]
    cp, sp = c[:NPAIR], s[:NPAIR]
    for m in range(1, WMAX + 1):
        cz, sz = c[NPAIR + m : NPAIR + m + 1], s[NPAIR + m : NPAIR + m + 1]
        cc, ss, sc, cs = cp * cz, sp * sz, sp * cz, cp * sz
        cos_parts.append(jnp.concatenate([cc - ss, cc + ss], axis=0).astype(BF16))
        sin_parts.append(jnp.concatenate([sc + cs, sc - cs], axis=0).astype(BF16))
    return jnp.concatenate(cos_parts + sin_parts, axis=0)


def coords16(xyz):
    return jnp.concatenate(
        [xyz.astype(F32), jnp.zeros((COORD_ROWS - 3, xyz.shape[1]), F32)], axis=0
    ).astype(BF16)


def split3(v):
    hi = v.astype(BF16).astype(F32)
    mid = (v - hi).astype(BF16).astype(F32)
    return hi, mid, (v - hi) - mid


def rows_near(xyz):
    x = xyz.astype(F32)
    hi, mid, lo = split3(jnp.sum(x * x, axis=0, keepdims=True))
    one = jnp.ones_like(hi)
    return jnp.concatenate(
        [-2.0 * x, hi, mid, lo, one, one, one, jnp.zeros((7, x.shape[1]), F32)], axis=0
    ).astype(BF16)


def rows_far(xyz):
    x = xyz.astype(F32)
    hi, mid, lo = split3(jnp.sum(x * x, axis=0, keepdims=True))
    one = jnp.ones_like(hi)
    return jnp.concatenate(
        [x, one, one, one, hi, mid, lo, jnp.zeros((7, x.shape[1]), F32)], axis=0
    ).astype(BF16)


def select_kernel(lists_ref, order_ref, feats_ref, coords_ref, *rest):
    outs = rest[:4]
    for slot in range(4):
        direction = order_ref[slot]
        pieces = []
        for h in range(HB):
            b = lists_ref[0, direction, h]
            start = pl.multiple_of(b * BLK, BLK)
            outs[slot][pl.ds(h * BLK, BLK), :] = feats_ref[pl.ds(start, BLK), :]
            pieces.append(coords_ref[:, pl.ds(start, BLK)].astype(F32))
            pieces.append(jnp.zeros((COORD_ROWS // HB - 3, BLK), F32))
        outs[slot][pl.ds(HB * BLK, COORD_ROWS), :] = jnp.concatenate(pieces, axis=0).astype(BF16)


def struct_kernel(chunk, flip_ref, feats_ref, coords_ref, w_ref, table_ref, keep_ref, send_ref, total_ref):
    atoms = feats_ref.shape[0]
    table = table_ref[...].astype(BF16)
    w = w_ref[...]
    for first in range(0, atoms, chunk):
        charges = dot(feats_ref[pl.ds(first, chunk), :], w).astype(BF16)
        trig = trig_chunk(table, coords16(coords_ref[:, pl.ds(first, chunk)]))
        part = dot(trig, charges)
        if first == 0:
            total_ref[...] = part
        else:
            total_ref[...] += part
    mine = pl.multiple_of(flip_ref[0] * HALF, 8)
    other = pl.multiple_of((1 - flip_ref[0]) * HALF, 8)
    keep_ref[...] = total_ref[pl.ds(mine, HALF), :]
    send_ref[...] = total_ref[pl.ds(other, HALF), :].astype(BF16)


def tile_kernel(
    unroll,
    order_ref,
    tiles_ref,
    count_ref,
    feats_ref,
    coords_ref,
    cot_ref,
    wa_ref,
    wb_ref,
    got0,
    got1,
    got2,
    got3,
    msg_ref,
    own_ref,
    held0,
    held1,
    held2,
    held3,
    proj_ref,
    cotp_ref,
    far_ref,
    near_ref,
    grad_ref,
):
    atoms = feats_ref.shape[0]
    nblk = atoms // BLK
    extent = nblk + 4 * HB
    gots = (got0, got1, got2, got3)
    helds = (held0, held1, held2, held3)
    wa, wb = wa_ref[...], wb_ref[...]
    w_cat = jnp.concatenate([wa.astype(F32).T, wb.astype(F32).T], axis=0).astype(BF16)
    w_side = jnp.concatenate([wa, wb], axis=0)

    def source_block(j, feats, xyz):
        both = dot(w_cat, feats, NT).astype(BF16)
        proj_ref[j, :, 0:BLK] = both[:BLK]
        proj_ref[j, :, BLK:] = both[BLK:]
        far_ref[j] = rows_far(xyz).astype(F32).T.astype(BF16)

    for b in range(nblk):
        xyz = coords_ref[:, b * BLK : (b + 1) * BLK]
        source_block(b, feats_ref[b * BLK : (b + 1) * BLK, :], xyz)
        near_ref[b] = rows_near(xyz)
        both = dot(cot_ref[b * BLK : (b + 1) * BLK, :], w_side, NT).astype(BF16)
        cotp_ref[b, 0:BLK, :] = both[:, :BLK]
        cotp_ref[b, BLK:, :] = both[:, BLK:]
    for slot in range(4):
        tail = gots[slot][HB * BLK : HB * BLK + COORD_ROWS, :].astype(F32)
        for h in range(HB):
            j = nblk + order_ref[slot + 4] * HB + h
            at = h * (COORD_ROWS // HB)
            source_block(j, gots[slot][h * BLK : (h + 1) * BLK, :], tail[at : at + 3])

    msg_ref[...] = jnp.zeros_like(msg_ref)
    grad_ref[...] = jnp.zeros_like(grad_ref)

    def group(first, width):
        idx = [(tiles_ref[0, first + u, 0], tiles_ref[0, first + u, 1]) for u in range(width)]
        kers = []
        for i, j in idx:
            d = dot(far_ref[j], near_ref[i])
            a = jnp.exp2(d * (-RADIAL_A * LOG2E))
            a2 = a * a
            b = (a2 * a2) * a
            kers.append((a.astype(BF16), b.astype(BF16)))
        for (i, j), (ka, kb) in zip(idx, kers):
            msg_ref[i] += dot(proj_ref[j], jnp.concatenate([ka, kb], axis=0))
            grad_ref[j] += dot(jnp.concatenate([ka, kb], axis=1), cotp_ref[i])

    count = count_ref[0]
    whole = count // unroll

    @pl.loop(0, whole)
    def _(step):
        group(step * unroll, unroll)

    @pl.loop(whole * unroll, count)
    def _(step):
        group(step, 1)

    for b in range(nblk):
        own_ref[b * BLK : (b + 1) * BLK, :] = grad_ref[b] * MSG_SCALE
    for slot in range(4):
        for h in range(HB):
            j = nblk + order_ref[slot + 4] * HB + h
            helds[slot][h * BLK : (h + 1) * BLK, :] = (grad_ref[j] * MSG_SCALE).astype(BF16)


def update_kernel(
    chunk,
    group_atoms,
    flip_ref,
    mine_ref,
    other_ref,
    wave_ref,
    norm2_ref,
    table_ref,
    feats_ref,
    coords_ref,
    msg_ref,
    w_long_ref,
    gain_ref,
    w_in_ref,
    w_out_ref,
    out_ref,
    mixw_ref,
):
    atoms, width = feats_ref.shape
    pick = (
        lax.broadcasted_iota(jnp.int32, (8, 3), 0) == lax.broadcasted_iota(jnp.int32, (8, 3), 1)
    ).astype(F32).astype(BF16)
    n = dot(pick, wave_ref[...].astype(F32).astype(BF16), NT)
    n0, n1, n2 = n[0:1], n[1:2], n[2:3]
    lead = jnp.where(n0 != 0.0, n0, jnp.where(n1 != 0.0, n1, n2))
    sign = jnp.where(lead < 0.0, -1.0, 1.0)
    n0, n1, n2 = n0 * sign, n1 * sign, n2 * sign
    pair = jnp.where(n0 == 0.0, n1 - 1.0, n0 * (2 * WMAX + 1) + n1 + (2.0 * WMAX - (2 * WMAX + 1)))
    shift = jnp.where(
        n2 == 0.0,
        0.0,
        BASE_ROWS
        + (jnp.abs(n2) - 1.0) * (2 * NPAIR)
        + jnp.where(n2 < 0.0, float(NPAIR), 0.0),
    )
    row = jnp.where((n0 == 0.0) & (n1 == 0.0), NPAIR + n2, pair + shift)
    same = lax.broadcasted_iota(jnp.int32, (HALF, row.shape[1]), 0) == row.astype(jnp.int32)
    times = jnp.sum(same.astype(F32), axis=1, keepdims=True)
    norm2 = norm2_ref[...]
    strength = times * (jnp.exp(-norm2 / 16.0) / (1.0 + norm2) * float(group_atoms) ** (-0.5))

    w_long_t = w_long_ref[...].astype(F32).T.astype(BF16)
    mine = flip_ref[0] == 0
    a, b = mine_ref[...].astype(F32), other_ref[...].astype(F32)
    cos_w = (strength * jnp.where(mine, a, b)).astype(BF16)
    sin_w = (strength * jnp.where(mine, b, a)).astype(BF16)
    mix_w = dot(w_long_t, jnp.concatenate([cos_w, sin_w], axis=0), NT).astype(BF16)

    table = table_ref[...].astype(BF16)
    gain = jnp.broadcast_to(gain_ref[...], (chunk, width)).T
    w_in_t = w_in_ref[...].astype(F32).T.astype(BF16)
    w_out_t = w_out_ref[...].astype(F32).T.astype(BF16)
    for first in range(0, atoms, chunk):
        trig = trig_chunk(table, coords16(coords_ref[:, pl.ds(first, chunk)]))
        mixed = dot(mix_w, trig)
        msg = jnp.concatenate(
            [msg_ref[(first // BLK) + i] for i in range(chunk // BLK)], axis=1
        )
        mixed = mixed + msg * MSG_SCALE + feats_ref[pl.ds(first, chunk), :].astype(F32).T
        scale = lax.rsqrt(jnp.mean(mixed * mixed, axis=0, keepdims=True) + 1e-06)
        normed = (mixed * scale * gain).astype(BF16)
        pre = dot(w_in_t, normed)
        hidden = (pre / (1.0 + jnp.exp(-pre))).astype(BF16)
        out = mixed + dot(w_out_t, hidden)
        out_ref[pl.ds(first, chunk), :] = out.T.astype(BF16)


def adjoint_kernel(lists_ref, order_ref, own_ref, r0, r1, r2, r3, out_ref):
    out_ref[...] = own_ref[...]
    for slot, ref in enumerate((r0, r1, r2, r3)):
        for h in range(HB):
            b = lists_ref[0, order_ref[slot], h]
            at = pl.ds(pl.multiple_of(b * BLK, BLK), BLK)
            out_ref[at, :] += ref[h * BLK : (h + 1) * BLK, :].astype(F32)


def call(kernel, outs, args, specs, scratch=(), flops=0, nbytes=0):
    single = not isinstance(outs, (list, tuple))
    return pl.pallas_call(
        kernel,
        out_shape=outs,
        in_specs=[pl.BlockSpec(memory_space=s) for s in specs],
        out_specs=pl.BlockSpec(memory_space=VMEM)
        if single
        else [pl.BlockSpec(memory_space=VMEM) for _ in outs],
        scratch_shapes=list(scratch),
        compiler_params=pltpu.CompilerParams(vmem_limit_bytes=40 * 1024 * 1024),
        cost_estimate=pl.CostEstimate(flops=flops, bytes_accessed=nbytes, transcendentals=0),
    )(*args)


def exchange(value, axis, partner):
    length = lax.axis_size(axis)
    return lax.ppermute(value, axis, [(i, partner(i) % length) for i in range(length)])


def body(
    feats,
    coords,
    msg_cot,
    send_list,
    tiles,
    tile_count,
    wavevec,
    w_rad_a,
    w_rad_b,
    w_charge,
    w_long,
    norm_gain,
    w_in,
    w_out,
):
    atoms, width = feats.shape
    nblk = atoms // BLK
    extent = nblk + 4 * HB
    domains = lax.axis_size("dom")
    parity = lax.axis_index("dom") % 2
    odd = parity.astype(jnp.int32)
    sds = jax.ShapeDtypeStruct

    order = jnp.stack([odd, 1 - odd, 2 + 0 * odd, 3 + 0 * odd, 1 - odd, odd, 2 + 0 * odd, 3 + 0 * odd])
    pairing = (
        ("dom", lambda i: i ^ 1, lambda i: i ^ 1),
        ("dom", lambda i: i + (1 if i % 2 else -1), lambda i: i + (1 if i % 2 else -1)),
        ("group", lambda i: i + 1, lambda i: i - 1),
        ("group", lambda i: i - 1, lambda i: i + 1),
    )

    sent = call(
        select_kernel,
        [sds((HB * BLK + COORD_ROWS, width), BF16)] * 4,
        (send_list, order, feats, coords),
        (SMEM, SMEM, VMEM, VMEM),
        nbytes=1 << 20,
    )
    got = [exchange(sent[s], pairing[s][0], pairing[s][1]) for s in range(4)]

    table = jnp.asarray(base_table())
    norm2 = jnp.asarray(grid_norm2())
    flip = odd.reshape(1)
    keep, send = call(
        functools.partial(struct_kernel, 256),
        [sds((HALF, width), F32), sds((HALF, width), BF16)],
        (flip, feats, coords, w_charge, table),
        (SMEM, VMEM, VMEM, VMEM, VMEM),
        scratch=[VMEM((2 * HALF, width), F32)],
        flops=2 * 2 * HALF * atoms * width,
        nbytes=1 << 20,
    )
    total = keep + exchange(send, "dom", lambda i: i ^ 1).astype(F32)
    step = 2
    while step < domains:
        total = total + exchange(total.astype(BF16), "dom", lambda i: i ^ step).astype(F32)
        step *= 2
    total = total.astype(BF16)
    other = exchange(total, "dom", lambda i: i ^ 1)

    msg, own, *held = call(
        functools.partial(tile_kernel, 4),
        [sds((nblk, width, BLK), F32), sds((atoms, width), F32)] + [sds((HB * BLK, width), BF16)] * 4,
        (order, tiles, tile_count, feats, coords, msg_cot, w_rad_a, w_rad_b, *got),
        (SMEM, SMEM, SMEM) + (VMEM,) * 9,
        scratch=[
            VMEM((extent, width, 2 * BLK), BF16),
            VMEM((nblk, 2 * BLK, width), BF16),
            VMEM((extent, BLK, COORD_ROWS), BF16),
            VMEM((nblk, COORD_ROWS, BLK), BF16),
            VMEM((extent, BLK, width), F32),
        ],
        flops=8 * tiles.shape[1] * BLK * BLK * width,
        nbytes=4 << 20,
    )
    back = [exchange(held[s], pairing[s][0], pairing[s][2]) for s in range(4)]

    new_feats = call(
        functools.partial(update_kernel, 256, atoms * domains),
        sds((atoms, width), BF16),
        (
            flip, total, other, wavevec, norm2, table, feats, coords, msg, w_long,
            norm_gain.reshape(1, width), w_in, w_out,
        ),
        (SMEM,) + (VMEM,) * 12,
        scratch=[VMEM((8, 128), F32)],
        flops=2 * 2 * HALF * atoms * width,
        nbytes=4 << 20,
    )
    adjoint = call(
        adjoint_kernel,
        sds((atoms, width), F32),
        (send_list, order, own, *back),
        (SMEM, SMEM) + (VMEM,) * 5,
        nbytes=2 << 20,
    )
    return (new_feats, adjoint)


def solution(mesh):
    split = ("group", "dom")
    return jax.shard_map(
        body,
        mesh=mesh,
        in_specs=(
            P(split, None),
            P(None, split),
            P(split, None),
            P(split, None, None),
            P(split, None, None),
            P(split),
            P(),
            P(),
            P(),
            P(),
            P(),
            P(),
            P(),
            P(),
        ),
        out_specs=(P(split, None), P(split, None)),
        check_vma=False,
    )
```

```python
import functools

import jax
import jax.numpy as jnp
import numpy as np
from jax import lax
from jax.experimental import pallas as pl
from jax.experimental.pallas import tpu as pltpu
from jax.sharding import PartitionSpec as P

BLK = 128
HB = 2
WMAX = 4
COORD_ROWS = 16

RADIAL_A = 6.0
MSG_SCALE = 1.0 / 32.0
LOG2E = 1.4426950408889634

NT = (((1,), (1,)), ((), ()))
NN = (((1,), (0,)), ((), ()))

VMEM = pltpu.VMEM
SMEM = pltpu.SMEM
BF16 = jnp.bfloat16
F32 = jnp.float32


def dot(a, b, dims=NN):
    return lax.dot_general(a, b, dims, preferred_element_type=F32)


PAIRS = [(0, b) for b in range(1, WMAX + 1)] + [
    (a, b) for a in range(1, WMAX + 1) for b in range(-WMAX, WMAX + 1)
]
NPAIR = len(PAIRS)
BASE_ROWS = 48
HALF = BASE_ROWS + WMAX * 2 * NPAIR


def base_table():
    rows = np.zeros((BASE_ROWS, COORD_ROWS), np.float32)
    for r, (a, b) in enumerate(PAIRS):
        rows[r, 0], rows[r, 1] = a, b
    for m in range(WMAX + 1):
        rows[NPAIR + m, 2] = m
    return rows


def grid_norm2():
    base = (base_table() ** 2).sum(1)
    parts = [base]
    for m in range(1, WMAX + 1):
        parts += [base[:NPAIR] + m * m] * 2
    return np.concatenate(parts).reshape(HALF, 1).astype(np.float32)


def taylor(first, count):
    coef, out = 1.0, []
    for k in range(1, first + 1):
        coef /= k
    power = first
    for _ in range(count):
        out.append(coef)
        coef = -coef / ((power + 1) * (power + 2))
        power += 2
    return out


SIN_COEF = [c * np.pi ** (2 * i + 1) for i, c in enumerate(taylor(1, 7))]
COS_COEF = [c * np.pi ** (2 * i) for i, c in enumerate(taylor(0, 8))]


def horner(z, coefs):
    acc = jnp.full_like(z, coefs[-1])
    for c in coefs[-2::-1]:
        acc = acc * z + c
    return acc


def cos_sin_turns(turns):
    r = turns - jnp.round(turns)
    z = r * r
    s = r * horner(z, SIN_COEF)
    c = horner(z, COS_COEF)
    return 1.0 - 2.0 * (s * s), 2.0 * (s * c)


def trig_chunk(table, xyz16):
    c, s = cos_sin_turns(dot(table, xyz16))
    cos_parts, sin_parts = [c.astype(BF16)], [s.astype(BF16)]
    cp, sp = c[:NPAIR], s[:NPAIR]
    for m in range(1, WMAX + 1):
        cz, sz = c[NPAIR + m : NPAIR + m + 1], s[NPAIR + m : NPAIR + m + 1]
        cc, ss, sc, cs = cp * cz, sp * sz, sp * cz, cp * sz
        cos_parts.append(jnp.concatenate([cc - ss, cc + ss], axis=0).astype(BF16))
        sin_parts.append(jnp.concatenate([sc + cs, sc - cs], axis=0).astype(BF16))
    return jnp.concatenate(cos_parts + sin_parts, axis=0)


def coords16(xyz):
    return jnp.concatenate(
        [xyz.astype(F32), jnp.zeros((COORD_ROWS - 3, xyz.shape[1]), F32)], axis=0
    ).astype(BF16)


def split3(v):
    hi = v.astype(BF16).astype(F32)
    mid = (v - hi).astype(BF16).astype(F32)
    return hi, mid, (v - hi) - mid


def dist_rows(xyz, near):
    x = xyz.astype(F32)
    hi, mid, lo = split3(jnp.sum(x * x, axis=0, keepdims=True))
    one = jnp.ones_like(hi)
    rest = jnp.zeros((COORD_ROWS - 9, x.shape[1]), F32)
    if near:
        parts = [-2.0 * x, hi, mid, lo, one, one, one, rest]
    else:
        parts = [x, one, one, one, hi, mid, lo, rest]
    return jnp.concatenate(parts, axis=0)


def block(ref, b):
    return ref[b * BLK : (b + 1) * BLK, :]


def load_kernel(n_load, flip_ref, lists_hbm, *refs):
    sources, loaded = refs[:n_load], refs[n_load : 2 * n_load]
    outs, lists_ref, sems = refs[2 * n_load : 2 * n_load + 4], refs[-2], refs[-1]
    copies = [
        pltpu.make_async_copy(src, dst, sems.at[k])
        for k, (src, dst) in enumerate(zip((lists_hbm, *sources), (lists_ref, *loaded)))
    ]
    for copy in copies:
        copy.start()
    for copy in copies[:3]:
        copy.wait()
    feats_ref, coords_ref = loaded[0], loaded[1]
    odd = flip_ref[0]
    for slot, direction in enumerate((odd, 1 - odd, 2, 3)):
        pieces = []
        for h in range(HB):
            b = lists_ref[0, h, direction]
            start = pl.multiple_of(b * BLK, BLK)
            outs[slot][pl.ds(h * BLK, BLK), :] = feats_ref[pl.ds(start, BLK), :]
            pieces.append(coords_ref[:, pl.ds(start, BLK)].astype(F32))
            pieces.append(jnp.zeros((COORD_ROWS // HB - 3, BLK), F32))
        outs[slot][pl.ds(HB * BLK, COORD_ROWS), :] = jnp.concatenate(pieces, axis=0).astype(BF16)
    for copy in copies[3:]:
        copy.wait()


def struct_kernel(
    chunk, flip_ref, feats_ref, coords_ref, w_ref, table_ref, first_ref, keep_ref, send_ref, trig_ref, total_ref
):
    atoms = feats_ref.shape[0]
    table = table_ref[...].astype(BF16)
    w = w_ref[...]
    for first in range(0, atoms, chunk):
        charges = dot(feats_ref[pl.ds(first, chunk), :], w).astype(BF16)
        trig = trig_chunk(table, coords16(coords_ref[:, pl.ds(first, chunk)]))
        trig_ref[:, pl.ds(first, chunk)] = trig
        part = dot(trig, charges)
        if first == 0:
            total_ref[...] = part
        else:
            total_ref[...] += part
    mine = pl.multiple_of(flip_ref[0] * HALF, 8)
    other = pl.multiple_of((1 - flip_ref[0]) * HALF, 8)
    keep_ref[...] = total_ref[pl.ds(mine, HALF), :]
    head = first_ref.shape[0]
    send_ref[0:head, :] = first_ref[...]
    send_ref[head:, :] = total_ref[pl.ds(other, HALF), :].astype(BF16)


def source_block(j, w_cat, feats, far, proj_ref, far_ref):
    both = dot(w_cat, feats, NT).astype(BF16)
    proj_ref[j, :, 0:BLK] = both[:BLK]
    proj_ref[j, :, BLK:] = both[BLK:]
    far_ref[j] = far.T.astype(BF16)


def both_transposed(wa_ref, wb_ref):
    return jnp.concatenate([wa_ref[...].astype(F32).T, wb_ref[...].astype(F32).T], axis=0).astype(BF16)


def local_kernel(
    feats_ref, coords_ref, cot_ref, wa_ref, wb_ref, after_ref, proj_ref, far_ref, near_ref, cotp_ref
):
    nblk = feats_ref.shape[0] // BLK
    w_cat = both_transposed(wa_ref, wb_ref)
    w_side = jnp.concatenate([wa_ref[...], wb_ref[...]], axis=0)
    near = dist_rows(coords_ref[...], True).astype(BF16)
    far = dist_rows(coords_ref[...], False)
    for b in range(nblk):
        at = slice(b * BLK, (b + 1) * BLK)
        source_block(b, w_cat, block(feats_ref, b), far[:, at], proj_ref, far_ref)
        near_ref[b] = near[:, at]
        both = dot(block(cot_ref, b), w_side, NT).astype(BF16)
        cotp_ref[b, 0:BLK, :] = both[:, :BLK]
        cotp_ref[b, BLK:, :] = both[:, BLK:]


def tile_range(
    unroll, first, last, count, tiles_ref, proj_ref, far_ref, near_ref, cotp_ref, msg_ref, grad_ref
):
    spare_i, spare_j = msg_ref.shape[0] - 1, grad_ref.shape[0] - 1
    slots = tiles_ref.shape[2]

    @pl.loop(first, last)
    def _(step):
        idx = []
        for u in range(unroll):
            t = step * unroll + u
            at = jnp.minimum(t, slots - 1)
            i, j, live = tiles_ref[0, 0, at], tiles_ref[0, 1, at], t < count
            idx.append((i, j, jnp.where(live, i, spare_i), jnp.where(live, j, spare_j)))
        kers = []
        for i, j, _, _ in idx:
            d = dot(far_ref[j], near_ref[i])
            a = jnp.exp2(d * (-RADIAL_A * LOG2E))
            a2 = a * a
            b = (a2 * a2) * a
            kers.append((a.astype(BF16), b.astype(BF16)))
        for (i, j, to_i, to_j), (ka, kb) in zip(idx, kers):
            msg_ref[to_i] += dot(proj_ref[j], jnp.concatenate([ka, kb], axis=0))
            grad_ref[to_j] += dot(jnp.concatenate([ka, kb], axis=1), cotp_ref[i])


def groups(count, unroll):
    return (count + unroll - 1) // unroll


def tiles_first_kernel(
    unroll,
    flip_ref,
    tiles_ref,
    count_ref,
    got0,
    got1,
    got2,
    got3,
    wa_ref,
    wb_ref,
    near_ref,
    cotp_ref,
    proj_in,
    far_in,
    after_ref,
    proj_ref,
    far_ref,
    msg_ref,
    grad_ref,
):
    nblk = near_ref.shape[0]
    w_cat = both_transposed(wa_ref, wb_ref)
    odd = flip_ref[0]
    for got, place in zip((got0, got1, got2, got3), (1 - odd, odd, 2, 3)):
        tail = got[HB * BLK : HB * BLK + COORD_ROWS, :].astype(F32)
        for h in range(HB):
            at = h * (COORD_ROWS // HB)
            far = dist_rows(tail[at : at + 3], False)
            source_block(nblk + place * HB + h, w_cat, block(got, h), far, proj_ref, far_ref)
    msg_ref[...] = jnp.zeros_like(msg_ref)
    grad_ref[...] = jnp.zeros_like(grad_ref)
    count = count_ref[0]
    last = groups(count, unroll) // 2
    tile_range(unroll, 0, last, count, tiles_ref, proj_ref, far_ref, near_ref, cotp_ref, msg_ref, grad_ref)


def tiles_second_kernel(
    unroll,
    flip_ref,
    tiles_ref,
    count_ref,
    proj_ref,
    far_ref,
    near_ref,
    cotp_ref,
    msg_in,
    grad_in,
    after_ref,
    msg_ref,
    grad_ref,
    held0,
    held1,
    held2,
    held3,
):
    nblk = near_ref.shape[0]
    count = count_ref[0]
    last = groups(count, unroll)
    tile_range(unroll, last // 2, last, count, tiles_ref, proj_ref, far_ref, near_ref, cotp_ref, msg_ref, grad_ref)
    odd = flip_ref[0]
    for held, place in zip((held0, held1, held2, held3), (1 - odd, odd, 2, 3)):
        for h in range(HB):
            held[h * BLK : (h + 1) * BLK, :] = (grad_ref[nblk + place * HB + h] * MSG_SCALE).astype(BF16)


def prepare_kernel(
    group_atoms,
    wave_ref,
    norm2_ref,
    w_long_ref,
    gain_ref,
    w_in_ref,
    w_out_ref,
    feats_ref,
    after_ref,
    strength_ref,
    w_long_t_ref,
    w_in_t_ref,
    w_out_t_ref,
    gain_t_ref,
    feats_t_ref,
):
    n = wave_ref[...].astype(F32)
    n0, n1, n2 = n[0:1], n[1:2], n[2:3]
    lead = jnp.where(n0 != 0.0, n0, jnp.where(n1 != 0.0, n1, n2))
    sign = jnp.where(lead < 0.0, -1.0, 1.0)
    n0, n1, n2 = n0 * sign, n1 * sign, n2 * sign
    pair = jnp.where(n0 == 0.0, n1 - 1.0, n0 * (2 * WMAX + 1) + n1 + (2.0 * WMAX - (2 * WMAX + 1)))
    shift = jnp.where(
        n2 == 0.0,
        0.0,
        BASE_ROWS
        + (jnp.abs(n2) - 1.0) * (2 * NPAIR)
        + jnp.where(n2 < 0.0, float(NPAIR), 0.0),
    )
    row = jnp.where((n0 == 0.0) & (n1 == 0.0), NPAIR + n2, pair + shift)
    same = lax.broadcasted_iota(jnp.int32, (HALF, row.shape[1]), 0) == row.astype(jnp.int32)
    times = jnp.sum(same.astype(F32), axis=1, keepdims=True)
    norm2 = norm2_ref[...]
    strength = times * (jnp.exp(-norm2 / 16.0) / (1.0 + norm2) * float(group_atoms) ** (-0.5))
    strength_ref[...] = jnp.broadcast_to(strength, strength_ref.shape)
    w_long_t_ref[...] = w_long_ref[...].astype(F32).T.astype(BF16)
    w_in_t_ref[...] = w_in_ref[...].astype(F32).T.astype(BF16)
    w_out_t_ref[...] = w_out_ref[...].astype(F32).T.astype(BF16)
    gain_t_ref[...] = jnp.broadcast_to(gain_ref[...], gain_t_ref.shape).T
    for b in range(feats_ref.shape[0] // BLK):
        feats_t_ref[:, b * BLK : (b + 1) * BLK] = block(feats_ref, b).astype(F32).T.astype(BF16)


def update_kernel(
    chunk,
    flip_ref,
    mine_ref,
    other_ref,
    strength_ref,
    trig_ref,
    feats_t_ref,
    msg_ref,
    w_long_t_ref,
    gain_t_ref,
    w_in_t_ref,
    w_out_t_ref,
    out_ref,
    done_ref,
):
    done_ref[...] = jnp.zeros_like(done_ref)
    atoms = feats_t_ref.shape[1]
    mine = flip_ref[0] == 0
    a = (strength_ref[...] * mine_ref[...].astype(F32)).astype(BF16)
    b = (strength_ref[...] * other_ref[HB * BLK :, :].astype(F32)).astype(BF16)
    weighted = jnp.concatenate([jnp.where(mine, a, b), jnp.where(mine, b, a)], axis=0)
    mix_w = dot(w_long_t_ref[...], weighted, NT).astype(BF16)
    gain = jnp.concatenate([gain_t_ref[...]] * (chunk // BLK), axis=1)
    w_in_t = w_in_t_ref[...]
    w_out_t = w_out_t_ref[...]
    for first in range(0, atoms, chunk):
        at = slice(first, first + chunk)
        msg = jnp.concatenate([msg_ref[(first // BLK) + i] for i in range(chunk // BLK)], axis=1)
        mixed = dot(mix_w, trig_ref[:, at]) + msg * MSG_SCALE + feats_t_ref[:, at].astype(F32)
        scale = lax.rsqrt(jnp.mean(mixed * mixed, axis=0, keepdims=True) + 1e-06)
        normed = (mixed * scale * gain).astype(BF16)
        pre = dot(w_in_t, normed)
        hidden = (pre / (1.0 + jnp.exp(-pre))).astype(BF16)
        out = mixed + dot(w_out_t, hidden)
        out_ref[at, :] = out.T.astype(BF16)


def adjoint_kernel(lists_ref, flip_ref, grad_ref, r0, r1, r2, r3, after_ref, out_ref):
    nblk = out_ref.shape[0] // BLK
    odd = flip_ref[0]
    for b in range(nblk):
        out_ref[b * BLK : (b + 1) * BLK, :] = grad_ref[b] * MSG_SCALE
    for ref, direction in zip((r0, r1, r2, r3), (odd, 1 - odd, 2, 3)):
        for h in range(HB):
            b = lists_ref[0, h, direction]
            at = pl.ds(pl.multiple_of(b * BLK, BLK), BLK)
            out_ref[at, :] += ref[h * BLK : (h + 1) * BLK, :].astype(F32)


def call(kernel, outs, args, specs, scratch=(), us=1.0, aliases=None):
    single = not isinstance(outs, (list, tuple))
    return pl.pallas_call(
        kernel,
        out_shape=outs,
        in_specs=[pl.BlockSpec(memory_space=s) for s in specs],
        out_specs=pl.BlockSpec(memory_space=VMEM)
        if single
        else [pl.BlockSpec(memory_space=VMEM) for _ in outs],
        scratch_shapes=list(scratch),
        input_output_aliases=aliases or {},
        compiler_params=pltpu.CompilerParams(vmem_limit_bytes=24 * 1024 * 1024),
        cost_estimate=pl.CostEstimate(
            flops=int(us * 1.1e9), bytes_accessed=int(us * 3.4e6), transcendentals=0
        ),
    )(*args)


def exchange(value, axis, partner):
    length = lax.axis_size(axis)
    return lax.ppermute(value, axis, [(i, partner(i) % length) for i in range(length)])


def body(
    feats,
    coords,
    msg_cot,
    send_list,
    tiles,
    tile_count,
    wavevec,
    w_rad_a,
    w_rad_b,
    w_charge,
    w_long,
    norm_gain,
    w_in,
    w_out,
):
    atoms, width = feats.shape
    nblk = atoms // BLK
    extent = nblk + 4 * HB
    hidden = w_in.shape[1]
    domains = lax.axis_size("dom")
    flip = (lax.axis_index("dom") % 2).astype(jnp.int32).reshape(1)
    sds = jax.ShapeDtypeStruct
    like = lambda x: sds(x.shape, x.dtype)
    unroll = 16

    near_pair = lambda i: i ^ 1
    far_pair = lambda i: i + (1 if i % 2 else -1)
    up = lambda i: i + 1
    down = lambda i: i - 1
    lists = jnp.swapaxes(send_list, 1, 2)
    tile_rows = jnp.swapaxes(tiles, 1, 2)
    table = jnp.asarray(base_table())
    norm2 = jnp.asarray(grid_norm2())

    loads = tuple(
        pltpu.with_memory_space_constraint(x, pltpu.HBM)
        for x in (feats, coords, msg_cot, table, w_charge)
    )
    loaded = call(
        functools.partial(load_kernel, len(loads)),
        [like(x) for x in loads] + [sds((HB * BLK + COORD_ROWS, width), BF16)] * 4,
        (flip, pltpu.with_memory_space_constraint(lists, pltpu.HBM), *loads),
        (SMEM,) + (pltpu.HBM,) * (1 + len(loads)),
        scratch=[SMEM(lists.shape, lists.dtype), pltpu.SemaphoreType.DMA((1 + len(loads),))],
        us=1.2,
    )
    feats, coords, msg_cot, table, w_charge = loaded[: len(loads)]
    sent = loaded[len(loads) :]
    got1 = exchange(sent[1], "dom", far_pair)
    got2 = exchange(sent[2], "group", up)
    got3 = exchange(sent[3], "group", down)

    keep, send, trig = call(
        functools.partial(struct_kernel, 256),
        [
            sds((HALF, width), F32),
            sds((HB * BLK + COORD_ROWS + HALF, width), BF16),
            sds((2 * HALF, atoms), BF16),
        ],
        (flip, feats, coords, w_charge, table, sent[0]),
        (SMEM,) + (VMEM,) * 5,
        scratch=[VMEM((2 * HALF, width), F32)],
        us=2.3,
    )
    got0 = exchange(send, "dom", near_pair)
    proj, far, near, cotp = call(
        local_kernel,
        [
            sds((extent, width, 2 * BLK), BF16),
            sds((extent, BLK, COORD_ROWS), BF16),
            sds((nblk, COORD_ROWS, BLK), BF16),
            sds((nblk, 2 * BLK, width), BF16),
        ],
        (feats, coords, msg_cot, w_rad_a, w_rad_b, send),
        (VMEM,) * 5 + (pl.ANY,),
        us=1.0,
    )
    total = keep + got0[HB * BLK + COORD_ROWS :].astype(F32)
    sums = [total.astype(BF16)]
    step = 2
    while step < domains:
        total = total + exchange(sums[-1], "dom", lambda i: i ^ step).astype(F32)
        sums.append(total.astype(BF16))
        step *= 2

    proj, far, msg, grad = call(
        functools.partial(tiles_first_kernel, unroll),
        [like(proj), like(far), sds((nblk + 1, width, BLK), F32), sds((extent + 1, BLK, width), F32)],
        (flip, tile_rows, tile_count, got0, got1, got2, got3, w_rad_a, w_rad_b, near, cotp, proj, far, sums[0]),
        (SMEM,) * 3 + (VMEM,) * 10 + (pl.ANY,),
        aliases={11: 0, 12: 1},
        us=3.5,
    )
    msg, grad, *held = call(
        functools.partial(tiles_second_kernel, unroll),
        [like(msg), like(grad)] + [sds((HB * BLK, width), BF16)] * 4,
        (flip, tile_rows, tile_count, proj, far, near, cotp, msg, grad, sums[min(1, len(sums) - 1)]),
        (SMEM,) * 3 + (VMEM,) * 6 + (pl.ANY,),
        aliases={7: 0, 8: 1},
        us=3.5,
    )
    back1 = exchange(held[1], "dom", far_pair)
    back2 = exchange(held[2], "group", down)
    back3 = exchange(held[3], "group", up)
    total = sums[-1]
    last = jnp.concatenate([held[0], total], axis=0)
    back0 = exchange(last, "dom", near_pair)

    strength, w_long_t, w_in_t, w_out_t, gain_t, feats_t = call(
        functools.partial(prepare_kernel, atoms * domains),
        [
            sds((HALF, width), F32),
            sds((width, width), BF16),
            sds((hidden, width), BF16),
            sds((width, hidden), BF16),
            sds((width, BLK), F32),
            sds((width, atoms), BF16),
        ],
        (wavevec.T, norm2, w_long, norm_gain.reshape(1, width), w_in, w_out, feats, last),
        (VMEM,) * 7 + (pl.ANY,),
        us=0.5,
    )
    new_feats, done = call(
        functools.partial(update_kernel, 256),
        [sds((atoms, width), BF16), sds((8, BLK), F32)],
        (flip, total, back0, strength, trig, feats_t, msg, w_long_t, gain_t, w_in_t, w_out_t),
        (SMEM,) + (VMEM,) * 10,
        us=3.4,
    )
    adjoint = call(
        adjoint_kernel,
        sds((atoms, width), F32),
        (lists, flip, grad, back0, back1, back2, back3, done),
        (SMEM, SMEM) + (VMEM,) * 5 + (pl.ANY,),
        us=1.6,
    )
    return (new_feats, adjoint)


def solution(mesh):
    split = ("group", "dom")
    return jax.shard_map(
        body,
        mesh=mesh,
        in_specs=(
            P(split, None),
            P(None, split),
            P(split, None),
            P(split, None, None),
            P(split, None, None),
            P(split),
            P(),
            P(),
            P(),
            P(),
            P(),
            P(),
            P(),
            P(),
        ),
        out_specs=(P(split, None), P(split, None)),
        check_vma=False,
    )
```

```python
import functools

import jax
import jax.numpy as jnp
import numpy as np
from jax import lax
from jax.experimental import pallas as pl
from jax.experimental.pallas import tpu as pltpu
from jax.sharding import PartitionSpec as P

BLK = 128
HB = 2
WMAX = 4
COORD_ROWS = 16

RADIAL_A = 6.0
MSG_SCALE = 1.0 / 32.0
LOG2E = 1.4426950408889634

NT = (((1,), (1,)), ((), ()))
NN = (((1,), (0,)), ((), ()))

VMEM = pltpu.VMEM
SMEM = pltpu.SMEM
BF16 = jnp.bfloat16
F32 = jnp.float32


def dot(a, b, dims=NN):
    return lax.dot_general(a, b, dims, preferred_element_type=F32)


PAIRS = [(0, b) for b in range(1, WMAX + 1)] + [
    (a, b) for a in range(1, WMAX + 1) for b in range(-WMAX, WMAX + 1)
]
NPAIR = len(PAIRS)
BASE_ROWS = 48
HALF = BASE_ROWS + WMAX * 2 * NPAIR


def base_table():
    rows = np.zeros((BASE_ROWS, COORD_ROWS), np.float32)
    for r, (a, b) in enumerate(PAIRS):
        rows[r, 0], rows[r, 1] = a, b
    for m in range(WMAX + 1):
        rows[NPAIR + m, 2] = m
    return rows


def grid_norm2():
    base = (base_table() ** 2).sum(1)
    parts = [base]
    for m in range(1, WMAX + 1):
        parts += [base[:NPAIR] + m * m] * 2
    return np.concatenate(parts).reshape(HALF, 1).astype(np.float32)


def taylor(first, count):
    coef, out = 1.0, []
    for k in range(1, first + 1):
        coef /= k
    power = first
    for _ in range(count):
        out.append(coef)
        coef = -coef / ((power + 1) * (power + 2))
        power += 2
    return out


SIN_COEF = [c * np.pi ** (2 * i + 1) for i, c in enumerate(taylor(1, 7))]
COS_COEF = [c * np.pi ** (2 * i) for i, c in enumerate(taylor(0, 8))]


def horner(z, coefs):
    acc = jnp.full_like(z, coefs[-1])
    for c in coefs[-2::-1]:
        acc = acc * z + c
    return acc


def cos_sin_turns(turns):
    r = turns - jnp.round(turns)
    z = r * r
    s = r * horner(z, SIN_COEF)
    c = horner(z, COS_COEF)
    return 1.0 - 2.0 * (s * s), 2.0 * (s * c)


def trig_chunk(table, xyz16):
    c, s = cos_sin_turns(dot(table, xyz16))
    cos_parts, sin_parts = [c.astype(BF16)], [s.astype(BF16)]
    cp, sp = c[:NPAIR], s[:NPAIR]
    for m in range(1, WMAX + 1):
        cz, sz = c[NPAIR + m : NPAIR + m + 1], s[NPAIR + m : NPAIR + m + 1]
        cc, ss, sc, cs = cp * cz, sp * sz, sp * cz, cp * sz
        cos_parts.append(jnp.concatenate([cc - ss, cc + ss], axis=0).astype(BF16))
        sin_parts.append(jnp.concatenate([sc + cs, sc - cs], axis=0).astype(BF16))
    return jnp.concatenate(cos_parts + sin_parts, axis=0)


def coords16(xyz):
    return jnp.concatenate(
        [xyz.astype(F32), jnp.zeros((COORD_ROWS - 3, xyz.shape[1]), F32)], axis=0
    ).astype(BF16)


def split3(v):
    hi = v.astype(BF16).astype(F32)
    mid = (v - hi).astype(BF16).astype(F32)
    return hi, mid, (v - hi) - mid


def dist_rows(xyz, near):
    x = xyz.astype(F32)
    hi, mid, lo = split3(jnp.sum(x * x, axis=0, keepdims=True))
    one = jnp.ones_like(hi)
    rest = jnp.zeros((COORD_ROWS - 9, x.shape[1]), F32)
    if near:
        parts = [-2.0 * x, hi, mid, lo, one, one, one, rest]
    else:
        parts = [x, one, one, one, hi, mid, lo, rest]
    return jnp.concatenate(parts, axis=0)


def block(ref, b):
    return ref[b * BLK : (b + 1) * BLK, :]


def send_block(lists_ref, direction, feats_ref, coords_ref, out_ref):
    pieces = []
    for h in range(HB):
        start = pl.multiple_of(lists_ref[0, h, direction] * BLK, BLK)
        out_ref[pl.ds(h * BLK, BLK), :] = feats_ref[pl.ds(start, BLK), :]
        pieces.append(coords_ref[:, pl.ds(start, BLK)].astype(F32))
        pieces.append(jnp.zeros((COORD_ROWS // HB - 3, BLK), F32))
    out_ref[pl.ds(HB * BLK, COORD_ROWS), :] = jnp.concatenate(pieces, axis=0).astype(BF16)


def load_kernel(n_load, flip_ref, lists_hbm, *refs):
    sources, loaded = refs[:n_load], refs[n_load : 2 * n_load]
    outs, lists_ref, sems = refs[2 * n_load : 2 * n_load + 4], refs[-2], refs[-1]
    copies = [
        pltpu.make_async_copy(src, dst, sems.at[k])
        for k, (src, dst) in enumerate(zip((lists_hbm, *sources), (lists_ref, *loaded)))
    ]
    for copy in copies:
        copy.start()
    for copy in copies[:3]:
        copy.wait()
    odd = flip_ref[0]
    for out_ref, direction in zip(outs, (odd, 1 - odd, 2, 3)):
        send_block(lists_ref, direction, loaded[0], loaded[1], out_ref)
    for copy in copies[3:]:
        copy.wait()


def struct_kernel(
    chunk, flip_ref, feats_ref, coords_ref, w_ref, table_ref, first_ref, keep_ref, send_ref, trig_ref, total_ref
):
    atoms = feats_ref.shape[0]
    table = table_ref[...].astype(BF16)
    w = w_ref[...]
    for first in range(0, atoms, chunk):
        at = slice(first, first + chunk)
        charges = dot(feats_ref[at, :], w).astype(BF16)
        trig = trig_chunk(table, coords16(coords_ref[:, at]))
        trig_ref[:, at] = trig
        part = dot(trig, charges)
        if first == 0:
            total_ref[...] = part
        else:
            total_ref[...] += part
    mine = pl.multiple_of(flip_ref[0] * HALF, 8)
    other = pl.multiple_of((1 - flip_ref[0]) * HALF, 8)
    keep_ref[...] = total_ref[pl.ds(mine, HALF), :]
    head = first_ref.shape[0]
    send_ref[0:head, :] = first_ref[...]
    send_ref[head:, :] = total_ref[pl.ds(other, HALF), :].astype(BF16)


def source_block(j, w_cat, feats, far, proj_ref, far_ref):
    both = (dot(w_cat, feats, NT) * MSG_SCALE).astype(BF16)
    proj_ref[j, :, 0:BLK] = both[:BLK]
    proj_ref[j, :, BLK:] = both[BLK:]
    far_ref[j] = far.T.astype(BF16)


def both_transposed(wa_ref, wb_ref):
    return jnp.concatenate([wa_ref[...].astype(F32).T, wb_ref[...].astype(F32).T], axis=0).astype(BF16)


def halo_blocks(got, first_block, w_cat, proj_ref, far_ref):
    tail = got[HB * BLK : HB * BLK + COORD_ROWS, :].astype(F32)
    for h in range(HB):
        at = h * (COORD_ROWS // HB)
        far = dist_rows(tail[at : at + 3], False)
        source_block(first_block + h, w_cat, block(got, h), far, proj_ref, far_ref)


def tile_plan(tiles_ref, count_ref, nblk):
    slots = tiles_ref.shape[2]
    tiles = tiles_ref[0].astype(F32)
    iota = lambda axis: lax.broadcasted_iota(jnp.int32, (slots, slots), axis)
    before = (iota(1) < iota(0)).astype(F32).astype(BF16)
    same = (iota(1) == iota(0)).astype(F32).astype(BF16)
    number = lax.broadcasted_iota(jnp.int32, (1, slots), 1)
    live = (number < count_ref[...]).astype(F32)
    own = live * (tiles[1:2] < float(nblk)).astype(F32)
    parts = []
    for chosen in (own, live - own):
        row = jnp.broadcast_to(chosen, (8, slots)).astype(BF16)
        place = dot(before, row, NT)[:, 0:1].astype(jnp.int32)
        here = dot(same, row, NT)[:, 0:1] > 0.5
        move = ((iota(1) == place) & here).astype(F32).astype(BF16)
        moved = dot(jnp.concatenate([tiles, tiles, tiles, tiles], axis=0).astype(BF16), move)
        parts += [moved[0:2], jnp.broadcast_to(jnp.sum(chosen, axis=1, keepdims=True), (1, slots))]
    parts.append(jnp.zeros((2, slots), F32))
    return jnp.concatenate(parts, axis=0).astype(jnp.int32)


def local_kernel(
    tiles_ref,
    count_ref,
    feats_ref,
    coords_ref,
    cot_ref,
    wa_ref,
    wb_ref,
    flip_ref,
    got1,
    got2,
    got3,
    after_ref,
    proj_ref,
    far_ref,
    near_ref,
    cotp_ref,
    plan_ref,
):
    nblk = feats_ref.shape[0] // BLK
    plan_ref[...] = tile_plan(tiles_ref, count_ref, nblk)
    w_cat = both_transposed(wa_ref, wb_ref)
    w_side = jnp.concatenate([wa_ref[...], wb_ref[...]], axis=0)
    near = dist_rows(coords_ref[...], True).astype(BF16)
    far = dist_rows(coords_ref[...], False)
    for b in range(nblk):
        at = slice(b * BLK, (b + 1) * BLK)
        source_block(b, w_cat, block(feats_ref, b), far[:, at], proj_ref, far_ref)
        near_ref[b] = near[:, at]
        both = (dot(block(cot_ref, b), w_side, NT) * MSG_SCALE).astype(BF16)
        cotp_ref[b, 0:BLK, :] = both[:, :BLK]
        cotp_ref[b, BLK:, :] = both[:, BLK:]
    for got, place in zip((got1, got2, got3), (flip_ref[0], 2, 3)):
        halo_blocks(got, nblk + place * HB, w_cat, proj_ref, far_ref)


def tile_part(unroll, row, plan_ref, proj_ref, far_ref, near_ref, cotp_ref, msg_ref, grad_ref):
    spare_i, spare_j = msg_ref.shape[0] - 1, grad_ref.shape[0] - 1
    slots = plan_ref.shape[1]
    count = plan_ref[row + 2, 0]

    @pl.loop(0, (count + unroll - 1) // unroll)
    def _(step):
        idx = []
        for u in range(unroll):
            t = step * unroll + u
            at = jnp.minimum(t, slots - 1)
            i, j, live = plan_ref[row, at], plan_ref[row + 1, at], t < count
            idx.append((i, j, jnp.where(live, i, spare_i), jnp.where(live, j, spare_j)))
        kers = []
        for i, j, _, _ in idx:
            d = dot(far_ref[j], near_ref[i])
            a = jnp.exp2(d * (-RADIAL_A * LOG2E))
            a2 = a * a
            b = (a2 * a2) * a
            kers.append((a.astype(BF16), b.astype(BF16)))
        for (i, j, to_i, to_j), (ka, kb) in zip(idx, kers):
            msg_ref[to_i] += dot(proj_ref[j], jnp.concatenate([ka, kb], axis=0))
            grad_ref[to_j] += dot(jnp.concatenate([ka, kb], axis=1), cotp_ref[i])


def tiles_received_kernel(
    unroll,
    flip_ref,
    plan_ref,
    got0,
    wa_ref,
    wb_ref,
    near_ref,
    cotp_ref,
    proj_in,
    far_in,
    after_ref,
    proj_ref,
    far_ref,
    msg_ref,
    grad_ref,
    held0,
    held1,
    held2,
    held3,
):
    nblk = near_ref.shape[0]
    odd = flip_ref[0]
    halo_blocks(got0, nblk + (1 - odd) * HB, both_transposed(wa_ref, wb_ref), proj_ref, far_ref)
    msg_ref[...] = jnp.zeros_like(msg_ref)
    grad_ref[...] = jnp.zeros_like(grad_ref)
    tile_part(unroll, 3, plan_ref, proj_ref, far_ref, near_ref, cotp_ref, msg_ref, grad_ref)
    for held, place in zip((held0, held1, held2, held3), (1 - odd, odd, 2, 3)):
        for h in range(HB):
            held[h * BLK : (h + 1) * BLK, :] = grad_ref[nblk + place * HB + h].astype(BF16)


def tiles_own_kernel(
    unroll, plan_ref, proj_ref, far_ref, near_ref, cotp_ref, msg_in, grad_in, after_ref, msg_ref, grad_ref
):
    tile_part(unroll, 0, plan_ref, proj_ref, far_ref, near_ref, cotp_ref, msg_ref, grad_ref)


def prepare_kernel(
    group_atoms,
    flip_ref,
    wave_ref,
    norm2_ref,
    w_long_ref,
    gain_ref,
    w_in_ref,
    w_out_ref,
    feats_ref,
    after1,
    after2,
    after3,
    after4,
    strength_ref,
    w_long_t_ref,
    w_in_t_ref,
    w_out_t_ref,
    gain_t_ref,
    feats_t_ref,
    parity_ref,
):
    parity_ref[...] = jnp.full(parity_ref.shape, flip_ref[0].astype(F32))
    n = wave_ref[...].astype(F32)
    n0, n1, n2 = n[0:1], n[1:2], n[2:3]
    lead = jnp.where(n0 != 0.0, n0, jnp.where(n1 != 0.0, n1, n2))
    sign = jnp.where(lead < 0.0, -1.0, 1.0)
    n0, n1, n2 = n0 * sign, n1 * sign, n2 * sign
    pair = jnp.where(n0 == 0.0, n1 - 1.0, n0 * (2 * WMAX + 1) + n1 + (2.0 * WMAX - (2 * WMAX + 1)))
    shift = jnp.where(
        n2 == 0.0,
        0.0,
        BASE_ROWS
        + (jnp.abs(n2) - 1.0) * (2 * NPAIR)
        + jnp.where(n2 < 0.0, float(NPAIR), 0.0),
    )
    row = jnp.where((n0 == 0.0) & (n1 == 0.0), NPAIR + n2, pair + shift)
    same = lax.broadcasted_iota(jnp.int32, (HALF, row.shape[1]), 0) == row.astype(jnp.int32)
    times = jnp.sum(same.astype(F32), axis=1, keepdims=True)
    norm2 = norm2_ref[...]
    strength = times * (jnp.exp(-norm2 / 16.0) / (1.0 + norm2) * float(group_atoms) ** (-0.5))
    strength_ref[...] = jnp.broadcast_to(strength, strength_ref.shape)
    w_long_t_ref[...] = w_long_ref[...].astype(F32).T.astype(BF16)
    w_in_t_ref[...] = w_in_ref[...].astype(F32).T.astype(BF16)
    w_out_t_ref[...] = w_out_ref[...].astype(F32).T.astype(BF16)
    gain_t_ref[...] = jnp.broadcast_to(gain_ref[...], gain_t_ref.shape).T
    for b in range(feats_ref.shape[0] // BLK):
        feats_t_ref[:, b * BLK : (b + 1) * BLK] = block(feats_ref, b).astype(F32).T.astype(BF16)


def update_kernel(
    chunk,
    mine_ref,
    other_ref,
    strength_ref,
    trig_ref,
    feats_t_ref,
    msg_ref,
    w_long_t_ref,
    gain_t_ref,
    w_in_t_ref,
    w_out_t_ref,
    parity_ref,
    out_ref,
):
    atoms = feats_t_ref.shape[1]
    a = strength_ref[...] * mine_ref[...].astype(F32)
    b = strength_ref[...] * other_ref[HB * BLK :, :].astype(F32)
    even = parity_ref[0:1, :] == 0.0
    weighted = jnp.concatenate([jnp.where(even, a, b), jnp.where(even, b, a)], axis=0).astype(BF16)
    mix_w = dot(w_long_t_ref[...], weighted, NT).astype(BF16)
    gain = jnp.concatenate([gain_t_ref[...]] * (chunk // BLK), axis=1)
    w_in_t = w_in_t_ref[...]
    w_out_t = w_out_t_ref[...]
    for step in range(atoms // chunk):
        at = slice(step * chunk, (step + 1) * chunk)
        msg = jnp.concatenate([msg_ref[step * (chunk // BLK) + i] for i in range(chunk // BLK)], axis=1)
        mixed = dot(mix_w, trig_ref[:, at]) + msg + feats_t_ref[:, at].astype(F32)
        scale = lax.rsqrt(jnp.mean(mixed * mixed, axis=0, keepdims=True) + 1e-06)
        normed = (mixed * scale * gain).astype(BF16)
        pre = dot(w_in_t, normed)
        half = 0.5 * pre
        hidden = (half * jnp.tanh(half) + half).astype(BF16)
        out = mixed + dot(w_out_t, hidden)
        out_ref[at, :] = out.T.astype(BF16)


def finish_kernel(
    lists_ref,
    flip_ref,
    new_ref,
    back0,
    back1,
    back2,
    back3,
    grad_in,
    out_hbm,
    adjoint_hbm,
    grad_ref,
    sems,
):
    nblk = adjoint_hbm.shape[0]
    first = pltpu.make_async_copy(new_ref, out_hbm, sems.at[0])
    first.start()
    odd = flip_ref[0]
    for ref, direction in zip((back0, back1, back2, back3), (odd, 1 - odd, 2, 3)):
        for h in range(HB):
            grad_ref[lists_ref[0, h, direction]] += block(ref, h).astype(F32)
    second = pltpu.make_async_copy(grad_ref.at[pl.ds(0, nblk)], adjoint_hbm, sems.at[1])
    second.start()
    first.wait()
    second.wait()


def call(kernel, outs, args, specs, scratch=(), us=1.0, aliases=None, out_specs=None):
    return pl.pallas_call(
        kernel,
        out_shape=outs,
        in_specs=[pl.BlockSpec(memory_space=s) for s in specs],
        out_specs=[pl.BlockSpec(memory_space=s) for s in (out_specs or (VMEM,) * len(outs))],
        scratch_shapes=list(scratch),
        input_output_aliases=aliases or {},
        compiler_params=pltpu.CompilerParams(vmem_limit_bytes=24 * 1024 * 1024),
        cost_estimate=pl.CostEstimate(
            flops=int(us * 1.1e9), bytes_accessed=int(us * 3.4e6), transcendentals=0
        ),
    )(*args)


def exchange(value, axis, partner):
    length = lax.axis_size(axis)
    return lax.ppermute(value, axis, [(i, partner(i) % length) for i in range(length)])


def body(
    feats,
    coords,
    msg_cot,
    send_list,
    tiles,
    tile_count,
    wavevec,
    w_rad_a,
    w_rad_b,
    w_charge,
    w_long,
    norm_gain,
    w_in,
    w_out,
):
    atoms, width = feats.shape
    nblk = atoms // BLK
    extent = nblk + 4 * HB
    hidden = w_in.shape[1]
    domains = lax.axis_size("dom")
    flip = (lax.axis_index("dom") % 2).astype(jnp.int32).reshape(1)
    sds = jax.ShapeDtypeStruct
    like = lambda x: sds(x.shape, x.dtype)
    unroll = 16

    near_pair = lambda i: i ^ 1
    far_pair = lambda i: i + (1 if i % 2 else -1)
    up = lambda i: i + 1
    down = lambda i: i - 1
    lists = jnp.swapaxes(send_list, 1, 2)
    tile_rows = jnp.swapaxes(tiles, 1, 2)
    tile_count = tile_count.reshape(1, 1)
    table = jnp.asarray(base_table())
    norm2 = jnp.asarray(grid_norm2())

    in_hbm = lambda x: pltpu.with_memory_space_constraint(x, pltpu.HBM)
    loads = tuple(in_hbm(x) for x in (feats, coords, msg_cot, table, w_charge))
    loaded = call(
        functools.partial(load_kernel, len(loads)),
        [like(x) for x in loads] + [sds((HB * BLK + COORD_ROWS, width), BF16)] * 4,
        (flip, in_hbm(lists), *loads),
        (SMEM,) + (pltpu.HBM,) * (1 + len(loads)),
        scratch=[SMEM(lists.shape, lists.dtype), pltpu.SemaphoreType.DMA((1 + len(loads),))],
        us=1.2,
    )
    feats, coords, msg_cot, table, w_charge = loaded[: len(loads)]
    sent = loaded[len(loads) :]
    got1 = exchange(sent[1], "dom", far_pair)
    got2 = exchange(sent[2], "group", up)
    got3 = exchange(sent[3], "group", down)

    keep, send, trig = call(
        functools.partial(struct_kernel, 256),
        [
            sds((HALF, width), F32),
            sds((HB * BLK + COORD_ROWS + HALF, width), BF16),
            sds((2 * HALF, atoms), BF16),
        ],
        (flip, feats, coords, w_charge, table, sent[0]),
        (SMEM,) + (VMEM,) * 5,
        scratch=[VMEM((2 * HALF, width), F32)],
        us=2.3,
    )
    got0 = exchange(send, "dom", near_pair)
    total = keep + got0[HB * BLK + COORD_ROWS :].astype(F32)
    sums = [total.astype(BF16)]
    step = 2
    while step < domains:
        total = total + exchange(sums[-1], "dom", lambda i: i ^ step).astype(F32)
        sums.append(total.astype(BF16))
        step *= 2

    proj, far, near, cotp, plan = call(
        local_kernel,
        [
            sds((extent, width, 2 * BLK), BF16),
            sds((extent, BLK, COORD_ROWS), BF16),
            sds((nblk, COORD_ROWS, BLK), BF16),
            sds((nblk, 2 * BLK, width), BF16),
            sds((8, tiles.shape[1]), jnp.int32),
        ],
        (tile_rows, tile_count, feats, coords, msg_cot, w_rad_a, w_rad_b, flip, got1, got2, got3, send),
        (VMEM,) * 7 + (SMEM,) + (VMEM,) * 3 + (pl.ANY,),
        us=1.0,
    )
    proj, far, msg, grad, *held = call(
        functools.partial(tiles_received_kernel, unroll),
        [like(proj), like(far), sds((nblk + 1, width, BLK), F32), sds((extent + 1, BLK, width), F32)]
        + [sds((HB * BLK, width), BF16)] * 4,
        (flip, plan, got0, w_rad_a, w_rad_b, near, cotp, proj, far, sums[0]),
        (SMEM,) * 2 + (VMEM,) * 7 + (pl.ANY,),
        us=3.0,
        aliases={7: 0, 8: 1},
    )
    msg, grad = call(
        functools.partial(tiles_own_kernel, unroll),
        [like(msg), like(grad)],
        (plan, proj, far, near, cotp, msg, grad, sums[min(1, len(sums) - 1)]),
        (SMEM,) + (VMEM,) * 6 + (pl.ANY,),
        us=5.0,
        aliases={5: 0, 6: 1},
    )
    back1 = exchange(held[1], "dom", far_pair)
    back2 = exchange(held[2], "group", down)
    back3 = exchange(held[3], "group", up)
    total = sums[-1]
    back0 = exchange(jnp.concatenate([held[0], total], axis=0), "dom", near_pair)

    strength, w_long_t, w_in_t, w_out_t, gain_t, feats_t, parity = call(
        functools.partial(prepare_kernel, atoms * domains),
        [
            sds((HALF, width), F32),
            sds((width, width), BF16),
            sds((hidden, width), BF16),
            sds((width, hidden), BF16),
            sds((width, BLK), F32),
            sds((width, atoms), BF16),
            sds((8, width), F32),
        ],
        (flip, wavevec.T, norm2, w_long, norm_gain.reshape(1, width), w_in, w_out, feats, back1, back2, back3, msg),
        (SMEM,) + (VMEM,) * 7 + (pl.ANY,) * 4,
        us=0.5,
    )
    (new_feats,) = call(
        functools.partial(update_kernel, atoms // 2),
        [sds((atoms, width), BF16)],
        (total, back0, strength, trig, feats_t, msg, w_long_t, gain_t, w_in_t, w_out_t, parity),
        (VMEM,) * 11,
        us=2.5,
    )
    new_feats, adjoint, _ = call(
        finish_kernel,
        [sds((atoms, width), BF16), sds((nblk, BLK, width), F32), like(grad)],
        (lists, flip, new_feats, back0, back1, back2, back3, grad),
        (SMEM, SMEM) + (VMEM,) * 6,
        scratch=[pltpu.SemaphoreType.DMA((2,))],
        us=1.5,
        aliases={7: 2},
        out_specs=(pltpu.HBM, pltpu.HBM, VMEM),
    )
    return (new_feats, adjoint.reshape(atoms, width))


def solution(mesh):
    split = ("group", "dom")
    return jax.shard_map(
        body,
        mesh=mesh,
        in_specs=(
            P(split, None),
            P(None, split),
            P(split, None),
            P(split, None, None),
            P(split, None, None),
            P(split),
            P(),
            P(),
            P(),
            P(),
            P(),
            P(),
            P(),
            P(),
        ),
        out_specs=(P(split, None), P(split, None)),
        check_vma=False,
    )
```

```python
import functools

import jax
import jax.numpy as jnp
import numpy as np
from jax import lax
from jax.experimental import pallas as pl
from jax.experimental.pallas import tpu as pltpu
from jax.sharding import PartitionSpec as P

BLK = 128
HB = 2
WMAX = 4
COORD_ROWS = 16

RADIAL_A = 6.0
MSG_SCALE = 1.0 / 32.0
LOG2E = 1.4426950408889634

NT = (((1,), (1,)), ((), ()))
NN = (((1,), (0,)), ((), ()))

VMEM = pltpu.VMEM
SMEM = pltpu.SMEM
BF16 = jnp.bfloat16
F32 = jnp.float32


def dot(a, b, dims=NN):
    return lax.dot_general(a, b, dims, preferred_element_type=F32)


PAIRS = [(0, b) for b in range(1, WMAX + 1)] + [
    (a, b) for a in range(1, WMAX + 1) for b in range(-WMAX, WMAX + 1)
]
NPAIR = len(PAIRS)
BASE_ROWS = 48
HALF = BASE_ROWS + WMAX * 2 * NPAIR


def base_table():
    rows = np.zeros((BASE_ROWS, COORD_ROWS), np.float32)
    for r, (a, b) in enumerate(PAIRS):
        rows[r, 0], rows[r, 1] = a, b
    for m in range(WMAX + 1):
        rows[NPAIR + m, 2] = m
    return rows


def grid_norm2():
    base = (base_table() ** 2).sum(1)
    parts = [base]
    for m in range(1, WMAX + 1):
        parts += [base[:NPAIR] + m * m] * 2
    return np.concatenate(parts).reshape(HALF, 1).astype(np.float32)


def taylor(first, count):
    coef, out = 1.0, []
    for k in range(1, first + 1):
        coef /= k
    power = first
    for _ in range(count):
        out.append(coef)
        coef = -coef / ((power + 1) * (power + 2))
        power += 2
    return out


SIN_COEF = [c * np.pi ** (2 * i + 1) for i, c in enumerate(taylor(1, 7))]
COS_COEF = [c * np.pi ** (2 * i) for i, c in enumerate(taylor(0, 8))]


def horner(z, coefs):
    acc = jnp.full_like(z, coefs[-1])
    for c in coefs[-2::-1]:
        acc = acc * z + c
    return acc


def cos_sin_turns(turns):
    r = turns - jnp.round(turns)
    z = r * r
    s = r * horner(z, SIN_COEF)
    c = horner(z, COS_COEF)
    return 1.0 - 2.0 * (s * s), 2.0 * (s * c)


def trig_chunk(table, xyz16):
    c, s = cos_sin_turns(dot(table, xyz16))
    cos_parts, sin_parts = [c.astype(BF16)], [s.astype(BF16)]
    cp, sp = c[:NPAIR], s[:NPAIR]
    for m in range(1, WMAX + 1):
        cz, sz = c[NPAIR + m : NPAIR + m + 1], s[NPAIR + m : NPAIR + m + 1]
        cc, ss, sc, cs = cp * cz, sp * sz, sp * cz, cp * sz
        cos_parts.append(jnp.concatenate([cc - ss, cc + ss], axis=0).astype(BF16))
        sin_parts.append(jnp.concatenate([sc + cs, sc - cs], axis=0).astype(BF16))
    return jnp.concatenate(cos_parts + sin_parts, axis=0)


def coords16(xyz):
    return jnp.concatenate(
        [xyz.astype(F32), jnp.zeros((COORD_ROWS - 3, xyz.shape[1]), F32)], axis=0
    ).astype(BF16)


def split3(v):
    hi = v.astype(BF16).astype(F32)
    mid = (v - hi).astype(BF16).astype(F32)
    return hi, mid, (v - hi) - mid


def dist_rows(xyz, near):
    x = xyz.astype(F32)
    hi, mid, lo = split3(jnp.sum(x * x, axis=0, keepdims=True))
    one = jnp.ones_like(hi)
    rest = jnp.zeros((COORD_ROWS - 9, x.shape[1]), F32)
    if near:
        parts = [-2.0 * x, hi, mid, lo, one, one, one, rest]
    else:
        parts = [x, one, one, one, hi, mid, lo, rest]
    return jnp.concatenate(parts, axis=0)


def block(ref, b):
    return ref[b * BLK : (b + 1) * BLK, :]


def send_block(lists_ref, direction, feats_ref, coords_ref, out_ref):
    pieces = []
    for h in range(HB):
        start = pl.multiple_of(lists_ref[0, h, direction] * BLK, BLK)
        out_ref[pl.ds(h * BLK, BLK), :] = feats_ref[pl.ds(start, BLK), :]
        pieces.append(coords_ref[:, pl.ds(start, BLK)].astype(F32))
        pieces.append(jnp.zeros((COORD_ROWS // HB - 3, BLK), F32))
    out_ref[pl.ds(HB * BLK, COORD_ROWS), :] = jnp.concatenate(pieces, axis=0).astype(BF16)


def load_kernel(n_load, flip_ref, lists_hbm, *refs):
    sources, loaded = refs[:n_load], refs[n_load : 2 * n_load]
    outs, lists_ref, sems = refs[2 * n_load : 2 * n_load + 4], refs[-2], refs[-1]
    copies = [
        pltpu.make_async_copy(src, dst, sems.at[k])
        for k, (src, dst) in enumerate(zip((lists_hbm, *sources), (lists_ref, *loaded)))
    ]
    for copy in copies:
        copy.start()
    for copy in copies[:3]:
        copy.wait()
    odd = flip_ref[0]
    for out_ref, direction in zip(outs, (odd, 1 - odd, 2, 3)):
        send_block(lists_ref, direction, loaded[0], loaded[1], out_ref)
    for copy in copies[3:]:
        copy.wait()


def struct_kernel(
    chunk, flip_ref, feats_ref, coords_ref, w_ref, table_ref, first_ref, keep_ref, send_ref, trig_ref, total_ref
):
    atoms = feats_ref.shape[0]
    table = table_ref[...].astype(BF16)
    w = w_ref[...]
    for first in range(0, atoms, chunk):
        at = slice(first, first + chunk)
        charges = dot(feats_ref[at, :], w).astype(BF16)
        trig = trig_chunk(table, coords16(coords_ref[:, at]))
        trig_ref[:, at] = trig
        part = dot(trig, charges)
        if first == 0:
            total_ref[...] = part
        else:
            total_ref[...] += part
    mine = pl.multiple_of(flip_ref[0] * HALF, 8)
    other = pl.multiple_of((1 - flip_ref[0]) * HALF, 8)
    keep_ref[...] = total_ref[pl.ds(mine, HALF), :]
    head = first_ref.shape[0]
    send_ref[0:head, :] = first_ref[...]
    send_ref[head:, :] = total_ref[pl.ds(other, HALF), :].astype(BF16)


def source_block(j, w_cat, feats, far, proj_ref, far_ref):
    both = (dot(w_cat, feats, NT) * MSG_SCALE).astype(BF16)
    proj_ref[j, :, 0:BLK] = both[:BLK]
    proj_ref[j, :, BLK:] = both[BLK:]
    far_ref[j] = far.T.astype(BF16)


def both_transposed(wa_ref, wb_ref):
    return jnp.concatenate([wa_ref[...].astype(F32).T, wb_ref[...].astype(F32).T], axis=0).astype(BF16)


def halo_blocks(got, first_block, w_cat, proj_ref, far_ref):
    tail = got[HB * BLK : HB * BLK + COORD_ROWS, :].astype(F32)
    for h in range(HB):
        at = h * (COORD_ROWS // HB)
        far = dist_rows(tail[at : at + 3], False)
        source_block(first_block + h, w_cat, block(got, h), far, proj_ref, far_ref)


def tile_plan(tiles_ref, count_ref, nblk):
    slots = tiles_ref.shape[2]
    tiles = tiles_ref[0].astype(F32)
    iota = lambda axis: lax.broadcasted_iota(jnp.int32, (slots, slots), axis)
    before = (iota(1) < iota(0)).astype(F32).astype(BF16)
    same = (iota(1) == iota(0)).astype(F32).astype(BF16)
    number = lax.broadcasted_iota(jnp.int32, (1, slots), 1)
    live = (number < count_ref[...]).astype(F32)
    own = live * (tiles[1:2] < float(nblk)).astype(F32)
    parts = []
    for chosen in (own, live - own):
        row = jnp.broadcast_to(chosen, (8, slots)).astype(BF16)
        place = dot(before, row, NT)[:, 0:1].astype(jnp.int32)
        here = dot(same, row, NT)[:, 0:1] > 0.5
        move = ((iota(1) == place) & here).astype(F32).astype(BF16)
        moved = dot(jnp.concatenate([tiles, tiles, tiles, tiles], axis=0).astype(BF16), move)
        parts += [moved[0:2], jnp.broadcast_to(jnp.sum(chosen, axis=1, keepdims=True), (1, slots))]
    return parts


def local_kernel(
    feats_ref,
    coords_ref,
    cot_ref,
    wa_ref,
    wb_ref,
    after_ref,
    proj_ref,
    far_ref,
    near_ref,
    cotp_ref,
):
    nblk = feats_ref.shape[0] // BLK
    w_cat = both_transposed(wa_ref, wb_ref)
    w_side = jnp.concatenate([wa_ref[...], wb_ref[...]], axis=0)
    near = dist_rows(coords_ref[...], True).astype(BF16)
    far = dist_rows(coords_ref[...], False)
    for b in range(nblk):
        at = slice(b * BLK, (b + 1) * BLK)
        source_block(b, w_cat, block(feats_ref, b), far[:, at], proj_ref, far_ref)
        near_ref[b] = near[:, at]
        both = (dot(block(cot_ref, b), w_side, NT) * MSG_SCALE).astype(BF16)
        cotp_ref[b, 0:BLK, :] = both[:, :BLK]
        cotp_ref[b, BLK:, :] = both[:, BLK:]


def tile_part(unroll, row, plan_ref, proj_ref, far_ref, near_ref, cotp_ref, msg_ref, grad_ref):
    spare_i, spare_j = msg_ref.shape[0] - 1, grad_ref.shape[0] - 1
    slots = plan_ref.shape[1]
    count = plan_ref[row + 2, 0]

    def group(first, width):
        idx = []
        for u in range(width):
            t = first + u
            at = jnp.minimum(t, slots - 1)
            i, j, live = plan_ref[row, at], plan_ref[row + 1, at], t < count
            idx.append((i, j, jnp.where(live, i, spare_i), jnp.where(live, j, spare_j)))
        kers = []
        for i, j, _, _ in idx:
            d = dot(far_ref[j], near_ref[i])
            a = jnp.exp2(d * (-RADIAL_A * LOG2E))
            a2 = a * a
            b = (a2 * a2) * a
            kers.append((a.astype(BF16), b.astype(BF16)))
        for (i, j, to_i, to_j), (ka, kb) in zip(idx, kers):
            msg_ref[to_i] += dot(proj_ref[j], jnp.concatenate([ka, kb], axis=0))
            grad_ref[to_j] += dot(jnp.concatenate([ka, kb], axis=1), cotp_ref[i])

    half = unroll // 2
    whole = (count + half - 1) // unroll

    @pl.loop(0, whole)
    def _(step):
        group(step * unroll, unroll)

    @pl.when(count > whole * unroll)
    def _():
        group(whole * unroll, half)


def tiles_received_kernel(
    unroll,
    plan_vmem,
    got2,
    got3,
    got1,
    got0,
    wa_ref,
    wb_ref,
    near_ref,
    cotp_ref,
    proj_in,
    far_in,
    after_ref,
    proj_ref,
    far_ref,
    msg_ref,
    grad_ref,
    held0,
    held1,
    held2,
    held3,
    plan_ref,
    sem,
):
    copy = pltpu.make_async_copy(plan_vmem, plan_ref, sem)
    copy.start()
    nblk = near_ref.shape[0]
    w_cat = both_transposed(wa_ref, wb_ref)
    for got, place in ((got2, 2), (got3, 3)):
        halo_blocks(got, nblk + place * HB, w_cat, proj_ref, far_ref)
    msg_ref[...] = jnp.zeros_like(msg_ref)
    grad_ref[...] = jnp.zeros_like(grad_ref)
    copy.wait()
    odd = plan_ref[6, 0]
    places = (1 - odd, odd, 2, 3)
    for got, place in ((got0, 1 - odd), (got1, odd)):
        halo_blocks(got, nblk + place * HB, w_cat, proj_ref, far_ref)
    tile_part(unroll, 3, plan_ref, proj_ref, far_ref, near_ref, cotp_ref, msg_ref, grad_ref)
    for held, place in zip((held0, held1, held2, held3), places):
        for h in range(HB):
            held[h * BLK : (h + 1) * BLK, :] = grad_ref[nblk + place * HB + h].astype(BF16)


def tiles_own_kernel(
    unroll, plan_ref, proj_ref, far_ref, near_ref, cotp_ref, msg_in, grad_in, after_ref, msg_ref, grad_ref
):
    tile_part(unroll, 0, plan_ref, proj_ref, far_ref, near_ref, cotp_ref, msg_ref, grad_ref)


def prepare_kernel(
    group_atoms,
    lists_ref,
    flip_ref,
    tiles_ref,
    count_ref,
    wave_ref,
    norm2_ref,
    w_long_ref,
    gain_ref,
    w_in_ref,
    w_out_ref,
    feats_ref,
    keep_in,
    after_ref,
    strength_ref,
    w_long_t_ref,
    w_in_t_ref,
    w_out_t_ref,
    gain_t_ref,
    feats_t_ref,
    parity_ref,
    plan_ref,
    keep_ref,
):
    parts = tile_plan(tiles_ref, count_ref, feats_ref.shape[0] // BLK)
    lane = lax.broadcasted_iota(jnp.int32, (1, plan_ref.shape[1]), 1)
    blocks = jnp.zeros(lane.shape, jnp.int32)
    for direction in range(4):
        for h in range(HB):
            blocks = jnp.where(lane == direction * HB + h, lists_ref[0, h, direction], blocks)
    parts += [jnp.full(lane.shape, flip_ref[0].astype(F32)), blocks.astype(F32)]
    plan_ref[...] = jnp.concatenate(parts, axis=0).astype(jnp.int32)
    parity_ref[...] = jnp.full(parity_ref.shape, flip_ref[0].astype(F32))
    n = wave_ref[...].astype(F32)
    n0, n1, n2 = n[0:1], n[1:2], n[2:3]
    lead = jnp.where(n0 != 0.0, n0, jnp.where(n1 != 0.0, n1, n2))
    sign = jnp.where(lead < 0.0, -1.0, 1.0)
    n0, n1, n2 = n0 * sign, n1 * sign, n2 * sign
    pair = jnp.where(n0 == 0.0, n1 - 1.0, n0 * (2 * WMAX + 1) + n1 + (2.0 * WMAX - (2 * WMAX + 1)))
    shift = jnp.where(
        n2 == 0.0,
        0.0,
        BASE_ROWS
        + (jnp.abs(n2) - 1.0) * (2 * NPAIR)
        + jnp.where(n2 < 0.0, float(NPAIR), 0.0),
    )
    row = jnp.where((n0 == 0.0) & (n1 == 0.0), NPAIR + n2, pair + shift)
    same = lax.broadcasted_iota(jnp.int32, (HALF, row.shape[1]), 0) == row.astype(jnp.int32)
    times = jnp.sum(same.astype(F32), axis=1, keepdims=True)
    norm2 = norm2_ref[...]
    strength = times * (jnp.exp(-norm2 / 16.0) / (1.0 + norm2) * float(group_atoms) ** (-0.5))
    strength_ref[...] = jnp.broadcast_to(strength, strength_ref.shape)
    w_long_t_ref[...] = w_long_ref[...].astype(F32).T.astype(BF16)
    w_in_t_ref[...] = w_in_ref[...].astype(F32).T.astype(BF16)
    w_out_t_ref[...] = w_out_ref[...].astype(F32).T.astype(BF16)
    gain_t_ref[...] = jnp.broadcast_to(gain_ref[...], gain_t_ref.shape).T
    for b in range(feats_ref.shape[0] // BLK):
        feats_t_ref[:, b * BLK : (b + 1) * BLK] = block(feats_ref, b).astype(F32).T.astype(BF16)


def finish_kernel(
    chunk,
    plan_vmem,
    mine_ref,
    back2,
    back3,
    back1,
    back0,
    strength_ref,
    trig_ref,
    feats_t_ref,
    msg_ref,
    w_long_t_ref,
    gain_t_ref,
    w_in_t_ref,
    w_out_t_ref,
    parity_ref,
    grad_in,
    out_hbm,
    adjoint_hbm,
    grad_ref,
    out_ref,
    plan_ref,
    sems,
):
    plan_copy = pltpu.make_async_copy(plan_vmem, plan_ref, sems.at[1])
    plan_copy.start()
    copies = []
    atoms = feats_t_ref.shape[1]
    a = strength_ref[...] * mine_ref[...].astype(F32)
    b = strength_ref[...] * back0[HB * BLK :, :].astype(F32)
    even = parity_ref[0:1, :] == 0.0
    weighted = jnp.concatenate([jnp.where(even, a, b), jnp.where(even, b, a)], axis=0).astype(BF16)
    mix_w = dot(w_long_t_ref[...], weighted, NT).astype(BF16)
    gain = jnp.concatenate([gain_t_ref[...]] * (chunk // BLK), axis=1)
    w_in_t = w_in_t_ref[...]
    w_out_t = w_out_t_ref[...]
    for step in range(atoms // chunk):
        at = slice(step * chunk, (step + 1) * chunk)
        msg = jnp.concatenate([msg_ref[step * (chunk // BLK) + i] for i in range(chunk // BLK)], axis=1)
        mixed = dot(mix_w, trig_ref[:, at]) + msg + feats_t_ref[:, at].astype(F32)
        if step == 0:
            nblk = adjoint_hbm.shape[0]
            plan_copy.wait()
            odd = plan_ref[6, 0]
            for ref, direction in zip((back0, back1, back2, back3), (odd, 1 - odd, 2, 3)):
                for h in range(HB):
                    grad_ref[plan_ref[7, direction * HB + h]] += block(ref, h).astype(F32)
            copy = pltpu.make_async_copy(grad_ref.at[pl.ds(0, nblk)], adjoint_hbm, sems.at[0])
            copy.start()
            copies.append(copy)
        scale = lax.rsqrt(jnp.mean(mixed * mixed, axis=0, keepdims=True) + 1e-06)
        normed = (mixed * scale * gain).astype(BF16)
        pre = dot(w_in_t, normed)
        half = 0.5 * pre
        hidden = (half * jnp.tanh(half) + half).astype(BF16)
        out = mixed + dot(w_out_t, hidden)
        out_ref[at, :] = out.T.astype(BF16)
        rows = pl.ds(step * chunk, chunk)
        copy = pltpu.make_async_copy(out_ref.at[rows], out_hbm.at[rows], sems.at[2 + step])
        copy.start()
        copies.append(copy)
    for copy in copies:
        copy.wait()


def call(kernel, outs, args, specs, scratch=(), us=1.0, aliases=None, out_specs=None):
    return pl.pallas_call(
        kernel,
        out_shape=outs,
        in_specs=[pl.BlockSpec(memory_space=s) for s in specs],
        out_specs=[pl.BlockSpec(memory_space=s) for s in (out_specs or (VMEM,) * len(outs))],
        scratch_shapes=list(scratch),
        input_output_aliases=aliases or {},
        compiler_params=pltpu.CompilerParams(vmem_limit_bytes=24 * 1024 * 1024),
        cost_estimate=pl.CostEstimate(
            flops=int(us * 1.1e9), bytes_accessed=int(us * 3.4e6), transcendentals=0
        ),
    )(*args)


def exchange(value, axis, partner):
    length = lax.axis_size(axis)
    return lax.ppermute(value, axis, [(i, partner(i) % length) for i in range(length)])


def body(
    feats,
    coords,
    msg_cot,
    send_list,
    tiles,
    tile_count,
    wavevec,
    w_rad_a,
    w_rad_b,
    w_charge,
    w_long,
    norm_gain,
    w_in,
    w_out,
):
    atoms, width = feats.shape
    nblk = atoms // BLK
    extent = nblk + 4 * HB
    hidden = w_in.shape[1]
    domains = lax.axis_size("dom")
    flip = (lax.axis_index("dom") % 2).astype(jnp.int32).reshape(1)
    sds = jax.ShapeDtypeStruct
    like = lambda x: sds(x.shape, x.dtype)
    unroll = 16

    near_pair = lambda i: i ^ 1
    far_pair = lambda i: i + (1 if i % 2 else -1)
    up = lambda i: i + 1
    down = lambda i: i - 1
    lists = jnp.swapaxes(send_list, 1, 2)
    tile_rows = jnp.swapaxes(tiles, 1, 2)
    tile_count = tile_count.reshape(1, 1)
    table = jnp.asarray(base_table())
    norm2 = jnp.asarray(grid_norm2())

    in_hbm = lambda x: pltpu.with_memory_space_constraint(x, pltpu.HBM)
    loads = tuple(in_hbm(x) for x in (feats, coords, msg_cot, table, w_charge))
    loaded = call(
        functools.partial(load_kernel, len(loads)),
        [like(x) for x in loads] + [sds((HB * BLK + COORD_ROWS, width), BF16)] * 4,
        (flip, in_hbm(lists), *loads),
        (SMEM,) + (pltpu.HBM,) * (1 + len(loads)),
        scratch=[SMEM(lists.shape, lists.dtype), pltpu.SemaphoreType.DMA((1 + len(loads),))],
        us=1.2,
    )
    feats, coords, msg_cot, table, w_charge = loaded[: len(loads)]
    sent = loaded[len(loads) :]
    got2 = exchange(sent[2], "group", up)
    got3 = exchange(sent[3], "group", down)
    got1 = exchange(sent[1], "dom", far_pair)

    keep, send, trig = call(
        functools.partial(struct_kernel, 256),
        [
            sds((HALF, width), F32),
            sds((HB * BLK + COORD_ROWS + HALF, width), BF16),
            sds((2 * HALF, atoms), BF16),
        ],
        (flip, feats, coords, w_charge, table, sent[0]),
        (SMEM,) + (VMEM,) * 5,
        scratch=[VMEM((2 * HALF, width), F32)],
        us=0.1,
    )
    got0 = exchange(send, "dom", near_pair)
    strength, w_long_t, w_in_t, w_out_t, gain_t, feats_t, parity, plan, keep = call(
        functools.partial(prepare_kernel, atoms * domains),
        [
            sds((HALF, width), F32),
            sds((width, width), BF16),
            sds((hidden, width), BF16),
            sds((width, hidden), BF16),
            sds((width, BLK), F32),
            sds((width, atoms), BF16),
            sds((8, width), F32),
            sds((8, tiles.shape[1]), jnp.int32),
            like(keep),
        ],
        (
            lists, flip, tile_rows, tile_count, wavevec.T, norm2, w_long, norm_gain.reshape(1, width), w_in, w_out,
            feats, keep, send,
        ),
        (SMEM, SMEM) + (VMEM,) * 10 + (pl.ANY,),
        aliases={11: 8},
        us=0.1,
    )
    total = keep + got0[HB * BLK + COORD_ROWS :].astype(F32)
    sums = [total.astype(BF16)]
    step = 2
    while step < domains:
        total = total + exchange(sums[-1], "dom", lambda i: i ^ step).astype(F32)
        sums.append(total.astype(BF16))
        step *= 2

    proj, far, near, cotp = call(
        local_kernel,
        [
            sds((extent, width, 2 * BLK), BF16),
            sds((extent, BLK, COORD_ROWS), BF16),
            sds((nblk, COORD_ROWS, BLK), BF16),
            sds((nblk, 2 * BLK, width), BF16),
        ],
        (feats, coords, msg_cot, w_rad_a, w_rad_b, send),
        (VMEM,) * 5 + (pl.ANY,),
        us=0.1,
    )
    proj, far, msg, grad, *held = call(
        functools.partial(tiles_received_kernel, unroll),
        [like(proj), like(far), sds((nblk + 1, width, BLK), F32), sds((extent + 1, BLK, width), F32)]
        + [sds((HB * BLK, width), BF16)] * 4,
        (plan, got2, got3, got1, got0, w_rad_a, w_rad_b, near, cotp, proj, far, sums[0]),
        (VMEM,) * 11 + (pl.ANY,),
        scratch=[SMEM(plan.shape, plan.dtype), pltpu.SemaphoreType.DMA],
        us=3.0,
        aliases={9: 0, 10: 1},
    )
    msg, grad = call(
        functools.partial(tiles_own_kernel, unroll),
        [like(msg), like(grad)],
        (plan, proj, far, near, cotp, msg, grad, sums[min(1, len(sums) - 1)]),
        (SMEM,) + (VMEM,) * 6 + (pl.ANY,),
        us=5.0,
        aliases={5: 0, 6: 1},
    )
    back2 = exchange(held[2], "group", down)
    back3 = exchange(held[3], "group", up)
    back1 = exchange(held[1], "dom", far_pair)
    total = sums[-1]
    back0 = exchange(jnp.concatenate([held[0], total], axis=0), "dom", near_pair)

    chunk = atoms
    new_feats, adjoint, _ = call(
        functools.partial(finish_kernel, chunk),
        [sds((atoms, width), BF16), sds((nblk, BLK, width), F32), like(grad)],
        (
            plan, total, back2, back3, back1, back0, strength, trig, feats_t, msg, w_long_t, gain_t,
            w_in_t, w_out_t, parity, grad,
        ),
        (VMEM,) * 16,
        scratch=[
            VMEM((atoms, width), BF16),
            SMEM(plan.shape, plan.dtype),
            pltpu.SemaphoreType.DMA((2 + atoms // chunk,)),
        ],
        us=3.0,
        aliases={15: 2},
        out_specs=(pltpu.HBM, pltpu.HBM, VMEM),
    )
    return (new_feats, adjoint.reshape(atoms, width))


def solution(mesh):
    split = ("group", "dom")
    return jax.shard_map(
        body,
        mesh=mesh,
        in_specs=(
            P(split, None),
            P(None, split),
            P(split, None),
            P(split, None, None),
            P(split, None, None),
            P(split),
            P(),
            P(),
            P(),
            P(),
            P(),
            P(),
            P(),
            P(),
        ),
        out_specs=(P(split, None), P(split, None)),
        check_vma=False,
    )
```

```python
import functools

import jax
import jax.numpy as jnp
import numpy as np
from jax import lax
from jax.experimental import pallas as pl
from jax.experimental.pallas import tpu as pltpu
from jax.sharding import PartitionSpec as P

BLK = 128
HB = 2
WMAX = 4
COORD_ROWS = 16

RADIAL_A = 6.0
MSG_SCALE = 1.0 / 32.0
LOG2E = 1.4426950408889634

NT = (((1,), (1,)), ((), ()))
NN = (((1,), (0,)), ((), ()))

VMEM = pltpu.VMEM
SMEM = pltpu.SMEM
BF16 = jnp.bfloat16
F32 = jnp.float32


def dot(a, b, dims=NN):
    return lax.dot_general(a, b, dims, preferred_element_type=F32)


PAIRS = [(0, b) for b in range(1, WMAX + 1)] + [
    (a, b) for a in range(1, WMAX + 1) for b in range(-WMAX, WMAX + 1)
]
NPAIR = len(PAIRS)
BASE_ROWS = 48
HALF = BASE_ROWS + WMAX * 2 * NPAIR


def base_table():
    rows = np.zeros((BASE_ROWS, COORD_ROWS), np.float32)
    for r, (a, b) in enumerate(PAIRS):
        rows[r, 0], rows[r, 1] = a, b
    for m in range(WMAX + 1):
        rows[NPAIR + m, 2] = m
    return rows


def grid_norm2():
    base = (base_table() ** 2).sum(1)
    parts = [base]
    for m in range(1, WMAX + 1):
        parts += [base[:NPAIR] + m * m] * 2
    return np.concatenate(parts).reshape(HALF, 1).astype(np.float32)


def taylor(first, count):
    coef, out = 1.0, []
    for k in range(1, first + 1):
        coef /= k
    power = first
    for _ in range(count):
        out.append(coef)
        coef = -coef / ((power + 1) * (power + 2))
        power += 2
    return out


SIN_COEF = [c * np.pi ** (2 * i + 1) for i, c in enumerate(taylor(1, 7))]
COS_COEF = [c * np.pi ** (2 * i) for i, c in enumerate(taylor(0, 8))]


def horner(z, coefs):
    acc = jnp.full_like(z, coefs[-1])
    for c in coefs[-2::-1]:
        acc = acc * z + c
    return acc


def cos_sin_turns(turns):
    r = turns - jnp.round(turns)
    z = r * r
    s = r * horner(z, SIN_COEF)
    c = horner(z, COS_COEF)
    return 1.0 - 2.0 * (s * s), 2.0 * (s * c)


def trig_chunk(table, xyz16):
    c, s = cos_sin_turns(dot(table, xyz16))
    cos_parts, sin_parts = [c.astype(BF16)], [s.astype(BF16)]
    cp, sp = c[:NPAIR], s[:NPAIR]
    for m in range(1, WMAX + 1):
        cz, sz = c[NPAIR + m : NPAIR + m + 1], s[NPAIR + m : NPAIR + m + 1]
        cc, ss, sc, cs = cp * cz, sp * sz, sp * cz, cp * sz
        cos_parts.append(jnp.concatenate([cc - ss, cc + ss], axis=0).astype(BF16))
        sin_parts.append(jnp.concatenate([sc + cs, sc - cs], axis=0).astype(BF16))
    return jnp.concatenate(cos_parts + sin_parts, axis=0)


def coords16(xyz):
    return jnp.concatenate(
        [xyz.astype(F32), jnp.zeros((COORD_ROWS - 3, xyz.shape[1]), F32)], axis=0
    ).astype(BF16)


def split3(v):
    hi = v.astype(BF16).astype(F32)
    mid = (v - hi).astype(BF16).astype(F32)
    return hi, mid, (v - hi) - mid


def dist_rows(xyz, near):
    x = xyz.astype(F32)
    hi, mid, lo = split3(jnp.sum(x * x, axis=0, keepdims=True))
    one = jnp.ones_like(hi)
    rest = jnp.zeros((COORD_ROWS - 9, x.shape[1]), F32)
    if near:
        parts = [-2.0 * x, hi, mid, lo, one, one, one, rest]
    else:
        parts = [x, one, one, one, hi, mid, lo, rest]
    return jnp.concatenate(parts, axis=0)


def block(ref, b):
    return ref[b * BLK : (b + 1) * BLK, :]


def send_block(lists_ref, direction, feats_ref, coords_ref, out_ref):
    pieces = []
    for h in range(HB):
        start = pl.multiple_of(lists_ref[0, h, direction] * BLK, BLK)
        out_ref[pl.ds(h * BLK, BLK), :] = feats_ref[pl.ds(start, BLK), :]
        pieces.append(coords_ref[:, pl.ds(start, BLK)].astype(F32))
        pieces.append(jnp.zeros((COORD_ROWS // HB - 3, BLK), F32))
    out_ref[pl.ds(HB * BLK, COORD_ROWS), :] = jnp.concatenate(pieces, axis=0).astype(BF16)


def load_kernel(n_load, flip_ref, lists_hbm, *refs):
    sources, loaded = refs[:n_load], refs[n_load : 2 * n_load]
    outs, lists_ref, sems = refs[2 * n_load : 2 * n_load + 4], refs[-2], refs[-1]
    copies = [
        pltpu.make_async_copy(src, dst, sems.at[k])
        for k, (src, dst) in enumerate(zip((lists_hbm, *sources), (lists_ref, *loaded)))
    ]
    for copy in copies:
        copy.start()
    for copy in copies[:3]:
        copy.wait()
    odd = flip_ref[0]
    for out_ref, direction in zip(outs, (odd, 1 - odd, 2, 3)):
        send_block(lists_ref, direction, loaded[0], loaded[1], out_ref)
    for copy in copies[3:]:
        copy.wait()


def struct_kernel(
    chunk, flip_ref, feats_ref, coords_ref, w_ref, table_ref, first_ref, keep_ref, send_ref, trig_ref, total_ref
):
    atoms = feats_ref.shape[0]
    table = table_ref[...].astype(BF16)
    w = w_ref[...]
    for first in range(0, atoms, chunk):
        at = slice(first, first + chunk)
        charges = dot(feats_ref[at, :], w).astype(BF16)
        trig = trig_chunk(table, coords16(coords_ref[:, at]))
        trig_ref[:, at] = trig
        part = dot(trig, charges)
        if first == 0:
            total_ref[...] = part
        else:
            total_ref[...] += part
    mine = pl.multiple_of(flip_ref[0] * HALF, 8)
    other = pl.multiple_of((1 - flip_ref[0]) * HALF, 8)
    keep_ref[...] = total_ref[pl.ds(mine, HALF), :]
    head = first_ref.shape[0]
    send_ref[0:head, :] = first_ref[...]
    send_ref[head:, :] = total_ref[pl.ds(other, HALF), :].astype(BF16)


def source_block(j, w_cat, feats, far, proj_ref, far_ref):
    both = (dot(w_cat, feats, NT) * MSG_SCALE).astype(BF16)
    proj_ref[j, :, 0:BLK] = both[:BLK]
    proj_ref[j, :, BLK:] = both[BLK:]
    far_ref[j] = far.T.astype(BF16)


def both_transposed(wa_ref, wb_ref):
    return jnp.concatenate([wa_ref[...].astype(F32).T, wb_ref[...].astype(F32).T], axis=0).astype(BF16)


def halo_blocks(got, first_block, w_cat, proj_ref, far_ref):
    tail = got[HB * BLK : HB * BLK + COORD_ROWS, :].astype(F32)
    for h in range(HB):
        at = h * (COORD_ROWS // HB)
        far = dist_rows(tail[at : at + 3], False)
        source_block(first_block + h, w_cat, block(got, h), far, proj_ref, far_ref)


def tile_plan(tiles_ref, count_ref, nblk):
    slots = tiles_ref.shape[2]
    tiles = tiles_ref[0].astype(F32)
    iota = lambda axis: lax.broadcasted_iota(jnp.int32, (slots, slots), axis)
    before = (iota(1) < iota(0)).astype(F32).astype(BF16)
    same = (iota(1) == iota(0)).astype(F32).astype(BF16)
    number = lax.broadcasted_iota(jnp.int32, (1, slots), 1)
    live = (number < count_ref[...]).astype(F32)
    own = live * (tiles[1:2] < float(nblk)).astype(F32)
    sub = lax.broadcasted_iota(jnp.int32, (8, slots), 0)
    rows = jnp.where(sub == 0, own, jnp.where(sub == 1, live - own, 0.0)).astype(BF16)
    columns = dot(jnp.concatenate([before, same], axis=0), rows, NT)
    counts = dot(rows, jnp.ones((slots, slots), BF16))
    both = jnp.where(sub % 2 == 0, tiles[0:1], tiles[1:2]).astype(BF16)
    parts = []
    for k in range(2):
        place = columns[:slots, k : k + 1].astype(jnp.int32)
        here = columns[slots:, k : k + 1] > 0.5
        moved = dot(both, ((iota(1) == place) & here).astype(F32).astype(BF16))
        parts += [moved[0:2], counts[k : k + 1]]
    return parts


def local_kernel(
    feats_ref,
    coords_ref,
    cot_ref,
    wa_ref,
    wb_ref,
    after_ref,
    proj_ref,
    far_ref,
    near_ref,
    cotp_ref,
):
    nblk = feats_ref.shape[0] // BLK
    w_cat = both_transposed(wa_ref, wb_ref)
    w_side = jnp.concatenate([wa_ref[...], wb_ref[...]], axis=0)
    near = dist_rows(coords_ref[...], True).astype(BF16)
    far = dist_rows(coords_ref[...], False)
    for b in range(nblk):
        at = slice(b * BLK, (b + 1) * BLK)
        source_block(b, w_cat, block(feats_ref, b), far[:, at], proj_ref, far_ref)
        near_ref[b] = near[:, at]
        both = (dot(block(cot_ref, b), w_side, NT) * MSG_SCALE).astype(BF16)
        cotp_ref[b, 0:BLK, :] = both[:, :BLK]
        cotp_ref[b, BLK:, :] = both[:, BLK:]


def tile_part(unroll, row, plan_ref, proj_ref, far_ref, near_ref, cotp_ref, msg_ref, grad_ref):
    spare_i, spare_j = msg_ref.shape[0] - 1, grad_ref.shape[0] - 1
    slots = plan_ref.shape[1]
    count = plan_ref[row + 2, 0]

    def group(first, width):
        idx = []
        for u in range(width):
            t = first + u
            at = jnp.minimum(t, slots - 1)
            i, j, live = plan_ref[row, at], plan_ref[row + 1, at], t < count
            idx.append((i, j, jnp.where(live, i, spare_i), jnp.where(live, j, spare_j)))
        kers = []
        for i, j, _, _ in idx:
            d = dot(far_ref[j], near_ref[i])
            a = jnp.exp2(d * (-RADIAL_A * LOG2E))
            a2 = a * a
            b = (a2 * a2) * a
            kers.append((a.astype(BF16), b.astype(BF16)))
        for (i, j, to_i, to_j), (ka, kb) in zip(idx, kers):
            msg_ref[to_i] += dot(proj_ref[j], jnp.concatenate([ka, kb], axis=0))
            grad_ref[to_j] += dot(jnp.concatenate([ka, kb], axis=1), cotp_ref[i])

    half = unroll // 2
    whole = (count + half - 1) // unroll

    @pl.loop(0, whole)
    def _(step):
        group(step * unroll, unroll)

    @pl.when(count > whole * unroll)
    def _():
        group(whole * unroll, half)


def tiles_received_kernel(
    unroll,
    plan_vmem,
    got2,
    got3,
    got1,
    got0,
    wa_ref,
    wb_ref,
    near_ref,
    cotp_ref,
    proj_in,
    far_in,
    after_ref,
    proj_ref,
    far_ref,
    msg_ref,
    grad_ref,
    held0,
    held1,
    held2,
    held3,
    plan_ref,
    sem,
):
    copy = pltpu.make_async_copy(plan_vmem, plan_ref, sem)
    copy.start()
    nblk = near_ref.shape[0]
    w_cat = both_transposed(wa_ref, wb_ref)
    for got, place in ((got2, 2), (got3, 3)):
        halo_blocks(got, nblk + place * HB, w_cat, proj_ref, far_ref)
    msg_ref[...] = jnp.zeros_like(msg_ref)
    grad_ref[...] = jnp.zeros_like(grad_ref)
    copy.wait()
    odd = plan_ref[6, 0]
    places = (1 - odd, odd, 2, 3)
    for got, place in ((got0, 1 - odd), (got1, odd)):
        halo_blocks(got, nblk + place * HB, w_cat, proj_ref, far_ref)
    tile_part(unroll, 3, plan_ref, proj_ref, far_ref, near_ref, cotp_ref, msg_ref, grad_ref)
    for held, place in zip((held0, held1, held2, held3), places):
        for h in range(HB):
            held[h * BLK : (h + 1) * BLK, :] = grad_ref[nblk + place * HB + h].astype(BF16)


def tiles_own_kernel(
    unroll, plan_ref, proj_ref, far_ref, near_ref, cotp_ref, msg_in, grad_in, after_ref, msg_ref, grad_ref
):
    tile_part(unroll, 0, plan_ref, proj_ref, far_ref, near_ref, cotp_ref, msg_ref, grad_ref)


def prepare_kernel(
    group_atoms,
    flip_ref,
    tiles_ref,
    count_ref,
    wave_ref,
    norm2_ref,
    w_long_ref,
    gain_ref,
    w_in_ref,
    w_out_ref,
    feats_ref,
    keep_in,
    after_ref,
    strength_ref,
    w_long_t_ref,
    w_in_t_ref,
    w_out_t_ref,
    gain_t_ref,
    feats_t_ref,
    parity_ref,
    plan_ref,
    keep_ref,
):
    parts = tile_plan(tiles_ref, count_ref, feats_ref.shape[0] // BLK)
    parts.append(jnp.full((2, plan_ref.shape[1]), flip_ref[0].astype(F32)))
    plan_ref[...] = jnp.concatenate(parts, axis=0).astype(jnp.int32)
    parity_ref[...] = jnp.full(parity_ref.shape, flip_ref[0].astype(F32))
    n = wave_ref[...].astype(F32)
    n0, n1, n2 = n[0:1], n[1:2], n[2:3]
    lead = jnp.where(n0 != 0.0, n0, jnp.where(n1 != 0.0, n1, n2))
    sign = jnp.where(lead < 0.0, -1.0, 1.0)
    n0, n1, n2 = n0 * sign, n1 * sign, n2 * sign
    pair = jnp.where(n0 == 0.0, n1 - 1.0, n0 * (2 * WMAX + 1) + n1 + (2.0 * WMAX - (2 * WMAX + 1)))
    shift = jnp.where(
        n2 == 0.0,
        0.0,
        BASE_ROWS
        + (jnp.abs(n2) - 1.0) * (2 * NPAIR)
        + jnp.where(n2 < 0.0, float(NPAIR), 0.0),
    )
    row = jnp.where((n0 == 0.0) & (n1 == 0.0), NPAIR + n2, pair + shift)
    same = lax.broadcasted_iota(jnp.int32, (HALF, row.shape[1]), 0) == row.astype(jnp.int32)
    times = jnp.sum(same.astype(F32), axis=1, keepdims=True)
    norm2 = norm2_ref[...]
    strength = times * (jnp.exp(-norm2 / 16.0) / (1.0 + norm2) * float(group_atoms) ** (-0.5))
    strength_ref[...] = jnp.broadcast_to(strength, strength_ref.shape)
    w_long_t_ref[...] = w_long_ref[...].astype(F32).T.astype(BF16)
    w_in_t_ref[...] = w_in_ref[...].astype(F32).T.astype(BF16)
    w_out_t_ref[...] = w_out_ref[...].astype(F32).T.astype(BF16)
    gain_t_ref[...] = jnp.broadcast_to(gain_ref[...], gain_t_ref.shape).T
    for b in range(feats_ref.shape[0] // BLK):
        feats_t_ref[:, b * BLK : (b + 1) * BLK] = block(feats_ref, b).astype(F32).T.astype(BF16)


def finish_kernel(
    chunk,
    lists_vmem,
    plan_vmem,
    mine_ref,
    back2,
    back3,
    back1,
    back0,
    strength_ref,
    trig_ref,
    feats_t_ref,
    msg_ref,
    w_long_t_ref,
    gain_t_ref,
    w_in_t_ref,
    w_out_t_ref,
    parity_ref,
    grad_in,
    out_hbm,
    adjoint_hbm,
    grad_ref,
    out_ref,
    lists_ref,
    plan_ref,
    sems,
):
    scalars = [
        pltpu.make_async_copy(lists_vmem, lists_ref, sems.at[1]),
        pltpu.make_async_copy(plan_vmem, plan_ref, sems.at[2]),
    ]
    for copy in scalars:
        copy.start()
    copies = []
    atoms = feats_t_ref.shape[1]
    a = strength_ref[...] * mine_ref[...].astype(F32)
    b = strength_ref[...] * back0[HB * BLK :, :].astype(F32)
    even = parity_ref[0:1, :] == 0.0
    weighted = jnp.concatenate([jnp.where(even, a, b), jnp.where(even, b, a)], axis=0).astype(BF16)
    mix_w = dot(w_long_t_ref[...], weighted, NT).astype(BF16)
    gain = jnp.concatenate([gain_t_ref[...]] * (chunk // BLK), axis=1)
    w_in_t = w_in_t_ref[...]
    w_out_t = w_out_t_ref[...]
    for step in range(atoms // chunk):
        at = slice(step * chunk, (step + 1) * chunk)
        msg = jnp.concatenate([msg_ref[step * (chunk // BLK) + i] for i in range(chunk // BLK)], axis=1)
        mixed = dot(mix_w, trig_ref[:, at]) + msg + feats_t_ref[:, at].astype(F32)
        if step == 0:
            nblk = adjoint_hbm.shape[0]
            for copy in scalars:
                copy.wait()
            odd = plan_ref[6, 0]
            for ref, direction in zip((back0, back1, back2, back3), (odd, 1 - odd, 2, 3)):
                for h in range(HB):
                    grad_ref[lists_ref[0, h, direction]] += block(ref, h).astype(F32)
            copy = pltpu.make_async_copy(grad_ref.at[pl.ds(0, nblk)], adjoint_hbm, sems.at[0])
            copy.start()
            copies.append(copy)
        scale = lax.rsqrt(jnp.mean(mixed * mixed, axis=0, keepdims=True) + 1e-06)
        normed = (mixed * scale * gain).astype(BF16)
        pre = dot(w_in_t, normed)
        half = 0.5 * pre
        hidden = (half * jnp.tanh(half) + half).astype(BF16)
        out = mixed + dot(w_out_t, hidden)
        out_ref[at, :] = out.T.astype(BF16)
        rows = pl.ds(step * chunk, chunk)
        copy = pltpu.make_async_copy(out_ref.at[rows], out_hbm.at[rows], sems.at[3 + step])
        copy.start()
        copies.append(copy)
    for copy in copies:
        copy.wait()


def call(kernel, outs, args, specs, scratch=(), us=1.0, aliases=None, out_specs=None):
    return pl.pallas_call(
        kernel,
        out_shape=outs,
        in_specs=[pl.BlockSpec(memory_space=s) for s in specs],
        out_specs=[pl.BlockSpec(memory_space=s) for s in (out_specs or (VMEM,) * len(outs))],
        scratch_shapes=list(scratch),
        input_output_aliases=aliases or {},
        compiler_params=pltpu.CompilerParams(vmem_limit_bytes=24 * 1024 * 1024),
        cost_estimate=pl.CostEstimate(
            flops=int(us * 1.1e9), bytes_accessed=int(us * 3.4e6), transcendentals=0
        ),
    )(*args)


def exchange(value, axis, partner):
    length = lax.axis_size(axis)
    return lax.ppermute(value, axis, [(i, partner(i) % length) for i in range(length)])


def body(
    feats,
    coords,
    msg_cot,
    send_list,
    tiles,
    tile_count,
    wavevec,
    w_rad_a,
    w_rad_b,
    w_charge,
    w_long,
    norm_gain,
    w_in,
    w_out,
):
    atoms, width = feats.shape
    nblk = atoms // BLK
    extent = nblk + 4 * HB
    hidden = w_in.shape[1]
    domains = lax.axis_size("dom")
    flip = (lax.axis_index("dom") % 2).astype(jnp.int32).reshape(1)
    sds = jax.ShapeDtypeStruct
    like = lambda x: sds(x.shape, x.dtype)
    unroll = 16

    near_pair = lambda i: i ^ 1
    far_pair = lambda i: i + (1 if i % 2 else -1)
    up = lambda i: i + 1
    down = lambda i: i - 1
    lists = jnp.swapaxes(send_list, 1, 2)
    tile_rows = jnp.swapaxes(tiles, 1, 2)
    tile_count = tile_count.reshape(1, 1)
    table = jnp.asarray(base_table())
    norm2 = jnp.asarray(grid_norm2())

    in_hbm = lambda x: pltpu.with_memory_space_constraint(x, pltpu.HBM)
    loads = tuple(in_hbm(x) for x in (feats, coords, msg_cot, table, w_charge))
    loaded = call(
        functools.partial(load_kernel, len(loads)),
        [like(x) for x in loads] + [sds((HB * BLK + COORD_ROWS, width), BF16)] * 4,
        (flip, in_hbm(lists), *loads),
        (SMEM,) + (pltpu.HBM,) * (1 + len(loads)),
        scratch=[SMEM(lists.shape, lists.dtype), pltpu.SemaphoreType.DMA((1 + len(loads),))],
        us=1.2,
    )
    feats, coords, msg_cot, table, w_charge = loaded[: len(loads)]
    sent = loaded[len(loads) :]
    got2 = exchange(sent[2], "group", up)
    got3 = exchange(sent[3], "group", down)
    got1 = exchange(sent[1], "dom", far_pair)

    keep, send, trig = call(
        functools.partial(struct_kernel, 256),
        [
            sds((HALF, width), F32),
            sds((HB * BLK + COORD_ROWS + HALF, width), BF16),
            sds((2 * HALF, atoms), BF16),
        ],
        (flip, feats, coords, w_charge, table, sent[0]),
        (SMEM,) + (VMEM,) * 5,
        scratch=[VMEM((2 * HALF, width), F32)],
        us=0.1,
    )
    got0 = exchange(send, "dom", near_pair)
    strength, w_long_t, w_in_t, w_out_t, gain_t, feats_t, parity, plan, keep = call(
        functools.partial(prepare_kernel, atoms * domains),
        [
            sds((HALF, width), F32),
            sds((width, width), BF16),
            sds((hidden, width), BF16),
            sds((width, hidden), BF16),
            sds((width, BLK), F32),
            sds((width, atoms), BF16),
            sds((8, width), F32),
            sds((8, tiles.shape[1]), jnp.int32),
            like(keep),
        ],
        (
            flip, tile_rows, tile_count, wavevec.T, norm2, w_long, norm_gain.reshape(1, width), w_in, w_out,
            feats, keep, send,
        ),
        (SMEM,) + (VMEM,) * 10 + (pl.ANY,),
        aliases={10: 8},
        us=0.1,
    )
    total = keep + got0[HB * BLK + COORD_ROWS :].astype(F32)
    sums = [total.astype(BF16)]
    step = 2
    while step < domains:
        total = total + exchange(sums[-1], "dom", lambda i: i ^ step).astype(F32)
        sums.append(total.astype(BF16))
        step *= 2

    proj, far, near, cotp = call(
        local_kernel,
        [
            sds((extent, width, 2 * BLK), BF16),
            sds((extent, BLK, COORD_ROWS), BF16),
            sds((nblk, COORD_ROWS, BLK), BF16),
            sds((nblk, 2 * BLK, width), BF16),
        ],
        (feats, coords, msg_cot, w_rad_a, w_rad_b, send),
        (VMEM,) * 5 + (pl.ANY,),
        us=0.1,
    )
    proj, far, msg, grad, *held = call(
        functools.partial(tiles_received_kernel, unroll),
        [like(proj), like(far), sds((nblk + 1, width, BLK), F32), sds((extent + 1, BLK, width), F32)]
        + [sds((HB * BLK, width), BF16)] * 4,
        (plan, got2, got3, got1, got0, w_rad_a, w_rad_b, near, cotp, proj, far, sums[0]),
        (VMEM,) * 11 + (pl.ANY,),
        scratch=[SMEM(plan.shape, plan.dtype), pltpu.SemaphoreType.DMA],
        us=3.0,
        aliases={9: 0, 10: 1},
    )
    msg, grad = call(
        functools.partial(tiles_own_kernel, unroll),
        [like(msg), like(grad)],
        (plan, proj, far, near, cotp, msg, grad, sums[min(1, len(sums) - 1)]),
        (SMEM,) + (VMEM,) * 6 + (pl.ANY,),
        us=5.0,
        aliases={5: 0, 6: 1},
    )
    back2 = exchange(held[2], "group", down)
    back3 = exchange(held[3], "group", up)
    back1 = exchange(held[1], "dom", far_pair)
    total = sums[-1]
    back0 = exchange(jnp.concatenate([held[0], total], axis=0), "dom", near_pair)

    chunk = atoms
    new_feats, adjoint, _ = call(
        functools.partial(finish_kernel, chunk),
        [sds((atoms, width), BF16), sds((nblk, BLK, width), F32), like(grad)],
        (
            lists, plan, total, back2, back3, back1, back0, strength, trig, feats_t, msg, w_long_t, gain_t,
            w_in_t, w_out_t, parity, grad,
        ),
        (VMEM,) * 17,
        scratch=[
            VMEM((atoms, width), BF16),
            SMEM(lists.shape, lists.dtype),
            SMEM(plan.shape, plan.dtype),
            pltpu.SemaphoreType.DMA((3 + atoms // chunk,)),
        ],
        us=3.0,
        aliases={16: 2},
        out_specs=(pltpu.HBM, pltpu.HBM, VMEM),
    )
    return (new_feats, adjoint.reshape(atoms, width))


def solution(mesh):
    split = ("group", "dom")
    return jax.shard_map(
        body,
        mesh=mesh,
        in_specs=(
            P(split, None),
            P(None, split),
            P(split, None),
            P(split, None, None),
            P(split, None, None),
            P(split),
            P(),
            P(),
            P(),
            P(),
            P(),
            P(),
            P(),
            P(),
        ),
        out_specs=(P(split, None), P(split, None)),
        check_vma=False,
    )
```

```python
import functools

import jax
import jax.numpy as jnp
import numpy as np
from jax import lax
from jax.experimental import pallas as pl
from jax.experimental.pallas import tpu as pltpu
from jax.sharding import PartitionSpec as P

BLK = 128
HB = 2
WMAX = 4
COORD_ROWS = 16

RADIAL_A = 6.0
MSG_SCALE = 1.0 / 32.0
LOG2E = 1.4426950408889634

NT = (((1,), (1,)), ((), ()))
NN = (((1,), (0,)), ((), ()))

VMEM = pltpu.VMEM
SMEM = pltpu.SMEM
BF16 = jnp.bfloat16
F32 = jnp.float32


def dot(a, b, dims=NN):
    return lax.dot_general(a, b, dims, preferred_element_type=F32)


PAIRS = [(0, b) for b in range(1, WMAX + 1)] + [
    (a, b) for a in range(1, WMAX + 1) for b in range(-WMAX, WMAX + 1)
]
NPAIR = len(PAIRS)
BASE_ROWS = 48
HALF = BASE_ROWS + WMAX * 2 * NPAIR


def base_table():
    rows = np.zeros((BASE_ROWS, COORD_ROWS), np.float32)
    for r, (a, b) in enumerate(PAIRS):
        rows[r, 0], rows[r, 1] = a, b
    for m in range(WMAX + 1):
        rows[NPAIR + m, 2] = m
    return rows


def grid_norm2():
    base = (base_table() ** 2).sum(1)
    parts = [base]
    for m in range(1, WMAX + 1):
        parts += [base[:NPAIR] + m * m] * 2
    return np.concatenate(parts).reshape(HALF, 1).astype(np.float32)


def taylor(first, count):
    coef, out = 1.0, []
    for k in range(1, first + 1):
        coef /= k
    power = first
    for _ in range(count):
        out.append(coef)
        coef = -coef / ((power + 1) * (power + 2))
        power += 2
    return out


SIN_COEF = [c * np.pi ** (2 * i + 1) for i, c in enumerate(taylor(1, 7))]
COS_COEF = [c * np.pi ** (2 * i) for i, c in enumerate(taylor(0, 8))]


def horner(z, coefs):
    acc = jnp.full_like(z, coefs[-1])
    for c in coefs[-2::-1]:
        acc = acc * z + c
    return acc


def cos_sin_turns(turns):
    r = turns - jnp.round(turns)
    z = r * r
    s = r * horner(z, SIN_COEF)
    c = horner(z, COS_COEF)
    return 1.0 - 2.0 * (s * s), 2.0 * (s * c)


def trig_chunk(table, xyz16):
    c, s = cos_sin_turns(dot(table, xyz16))
    cos_parts, sin_parts = [c.astype(BF16)], [s.astype(BF16)]
    cp, sp = c[:NPAIR], s[:NPAIR]
    for m in range(1, WMAX + 1):
        cz, sz = c[NPAIR + m : NPAIR + m + 1], s[NPAIR + m : NPAIR + m + 1]
        cc, ss, sc, cs = cp * cz, sp * sz, sp * cz, cp * sz
        cos_parts.append(jnp.concatenate([cc - ss, cc + ss], axis=0).astype(BF16))
        sin_parts.append(jnp.concatenate([sc + cs, sc - cs], axis=0).astype(BF16))
    return jnp.concatenate(cos_parts + sin_parts, axis=0)


def coords16(xyz):
    return jnp.concatenate(
        [xyz.astype(F32), jnp.zeros((COORD_ROWS - 3, xyz.shape[1]), F32)], axis=0
    ).astype(BF16)


def split3(v):
    hi = v.astype(BF16).astype(F32)
    mid = (v - hi).astype(BF16).astype(F32)
    return hi, mid, (v - hi) - mid


def dist_rows(xyz, near):
    x = xyz.astype(F32)
    hi, mid, lo = split3(jnp.sum(x * x, axis=0, keepdims=True))
    one = jnp.ones_like(hi)
    rest = jnp.zeros((COORD_ROWS - 9, x.shape[1]), F32)
    if near:
        parts = [-2.0 * x, hi, mid, lo, one, one, one, rest]
    else:
        parts = [x, one, one, one, hi, mid, lo, rest]
    return jnp.concatenate(parts, axis=0)


def block(ref, b):
    return ref[b * BLK : (b + 1) * BLK, :]


def send_block(lists_ref, direction, feats_ref, coords_ref, out_ref):
    pieces = []
    for h in range(HB):
        start = pl.multiple_of(lists_ref[0, h, direction] * BLK, BLK)
        out_ref[pl.ds(h * BLK, BLK), :] = feats_ref[pl.ds(start, BLK), :]
        pieces.append(coords_ref[:, pl.ds(start, BLK)].astype(F32))
        pieces.append(jnp.zeros((COORD_ROWS // HB - 3, BLK), F32))
    out_ref[pl.ds(HB * BLK, COORD_ROWS), :] = jnp.concatenate(pieces, axis=0).astype(BF16)


def load_kernel(n_load, flip_ref, lists_hbm, *refs):
    sources, loaded = refs[:n_load], refs[n_load : 2 * n_load]
    outs, lists_ref, sems = refs[2 * n_load : 2 * n_load + 4], refs[-2], refs[-1]
    copies = [
        pltpu.make_async_copy(src, dst, sems.at[k])
        for k, (src, dst) in enumerate(zip((lists_hbm, *sources), (lists_ref, *loaded)))
    ]
    for copy in copies:
        copy.start()
    for copy in copies[:3]:
        copy.wait()
    odd = flip_ref[0]
    for out_ref, direction in zip(outs, (odd, 1 - odd, 2, 3)):
        send_block(lists_ref, direction, loaded[0], loaded[1], out_ref)
    for copy in copies[3:]:
        copy.wait()


def struct_kernel(
    chunk, flip_ref, feats_ref, coords_ref, w_ref, table_ref, first_ref, keep_ref, send_ref, trig_ref, total_ref
):
    atoms = feats_ref.shape[0]
    table = table_ref[...].astype(BF16)
    w = w_ref[...]
    for first in range(0, atoms, chunk):
        at = slice(first, first + chunk)
        charges = dot(feats_ref[at, :], w).astype(BF16)
        trig = trig_chunk(table, coords16(coords_ref[:, at]))
        trig_ref[:, at] = trig
        part = dot(trig, charges)
        if first == 0:
            total_ref[...] = part
        else:
            total_ref[...] += part
    mine = pl.multiple_of(flip_ref[0] * HALF, 8)
    other = pl.multiple_of((1 - flip_ref[0]) * HALF, 8)
    keep_ref[...] = total_ref[pl.ds(mine, HALF), :]
    head = first_ref.shape[0]
    send_ref[0:head, :] = first_ref[...]
    send_ref[head:, :] = total_ref[pl.ds(other, HALF), :].astype(BF16)


def source_block(j, w_cat, feats, far, proj_ref, far_ref):
    both = (dot(w_cat, feats, NT) * MSG_SCALE).astype(BF16)
    proj_ref[j, :, 0:BLK] = both[:BLK]
    proj_ref[j, :, BLK:] = both[BLK:]
    far_ref[j] = far.T.astype(BF16)


def both_transposed(wa_ref, wb_ref):
    return jnp.concatenate([wa_ref[...].astype(F32).T, wb_ref[...].astype(F32).T], axis=0).astype(BF16)


def halo_blocks(got, first_block, w_cat, proj_ref, far_ref):
    tail = got[HB * BLK : HB * BLK + COORD_ROWS, :].astype(F32)
    for h in range(HB):
        at = h * (COORD_ROWS // HB)
        far = dist_rows(tail[at : at + 3], False)
        source_block(first_block + h, w_cat, block(got, h), far, proj_ref, far_ref)


def tile_plan(tiles_ref, count_ref, nblk):
    slots = tiles_ref.shape[2]
    tiles = tiles_ref[0].astype(F32)
    iota = lambda axis: lax.broadcasted_iota(jnp.int32, (slots, slots), axis)
    before = (iota(1) < iota(0)).astype(F32).astype(BF16)
    same = (iota(1) == iota(0)).astype(F32).astype(BF16)
    number = lax.broadcasted_iota(jnp.int32, (1, slots), 1)
    live = (number < count_ref[...]).astype(F32)
    own = live * (tiles[1:2] < float(nblk)).astype(F32)
    sub = lax.broadcasted_iota(jnp.int32, (8, slots), 0)
    rows = jnp.where(sub == 0, own, jnp.where(sub == 1, live - own, 0.0)).astype(BF16)
    columns = dot(jnp.concatenate([before, same], axis=0), rows, NT)
    counts = dot(rows, jnp.ones((slots, slots), BF16))
    both = jnp.where(sub % 2 == 0, tiles[0:1], tiles[1:2]).astype(BF16)
    parts = []
    for k in range(2):
        place = columns[:slots, k : k + 1].astype(jnp.int32)
        here = columns[slots:, k : k + 1] > 0.5
        moved = dot(both, ((iota(1) == place) & here).astype(F32).astype(BF16))
        parts += [moved[0:2], counts[k : k + 1]]
    return parts


def local_kernel(
    feats_ref,
    coords_ref,
    cot_ref,
    wa_ref,
    wb_ref,
    after_ref,
    proj_ref,
    far_ref,
    near_ref,
    cotp_ref,
):
    nblk = feats_ref.shape[0] // BLK
    w_cat = both_transposed(wa_ref, wb_ref)
    w_side = jnp.concatenate([wa_ref[...], wb_ref[...]], axis=0)
    near = dist_rows(coords_ref[...], True).astype(BF16)
    far = dist_rows(coords_ref[...], False)
    for b in range(nblk):
        at = slice(b * BLK, (b + 1) * BLK)
        source_block(b, w_cat, block(feats_ref, b), far[:, at], proj_ref, far_ref)
        near_ref[b] = near[:, at]
        both = (dot(block(cot_ref, b), w_side, NT) * MSG_SCALE).astype(BF16)
        cotp_ref[b, 0:BLK, :] = both[:, :BLK]
        cotp_ref[b, BLK:, :] = both[:, BLK:]


def tile_part(unroll, row, plan_ref, proj_ref, far_ref, near_ref, cotp_ref, msg_ref, grad_ref):
    spare_i, spare_j = msg_ref.shape[0] - 1, grad_ref.shape[0] - 1
    slots = plan_ref.shape[1]
    count = plan_ref[row + 2, 0]

    def group(first, width):
        idx = []
        for u in range(width):
            t = first + u
            at = jnp.minimum(t, slots - 1)
            i, j, live = plan_ref[row, at], plan_ref[row + 1, at], t < count
            idx.append((i, j, jnp.where(live, i, spare_i), jnp.where(live, j, spare_j)))
        kers = []
        for i, j, _, _ in idx:
            d = dot(far_ref[j], near_ref[i])
            a = jnp.exp2(d * (-RADIAL_A * LOG2E))
            a2 = a * a
            b = (a2 * a2) * a
            kers.append((a.astype(BF16), b.astype(BF16)))
        for (i, j, to_i, to_j), (ka, kb) in zip(idx, kers):
            msg_ref[to_i] += dot(proj_ref[j], jnp.concatenate([ka, kb], axis=0))
            grad_ref[to_j] += dot(jnp.concatenate([ka, kb], axis=1), cotp_ref[i])

    half = unroll // 2
    whole = (count + half - 1) // unroll

    @pl.loop(0, whole)
    def _(step):
        group(step * unroll, unroll)

    @pl.when(count > whole * unroll)
    def _():
        group(whole * unroll, half)


def tiles_received_kernel(
    unroll,
    plan_vmem,
    got1,
    got2,
    got3,
    got0,
    wa_ref,
    wb_ref,
    near_ref,
    cotp_ref,
    proj_in,
    far_in,
    after_ref,
    proj_ref,
    far_ref,
    msg_ref,
    grad_ref,
    held0,
    held1,
    held2,
    held3,
    plan_ref,
    sem,
):
    copy = pltpu.make_async_copy(plan_vmem, plan_ref, sem)
    copy.start()
    nblk = near_ref.shape[0]
    w_cat = both_transposed(wa_ref, wb_ref)
    for got, place in ((got2, 2), (got3, 3)):
        halo_blocks(got, nblk + place * HB, w_cat, proj_ref, far_ref)
    msg_ref[...] = jnp.zeros_like(msg_ref)
    grad_ref[...] = jnp.zeros_like(grad_ref)
    copy.wait()
    odd = plan_ref[6, 0]
    places = (1 - odd, odd, 2, 3)
    for got, place in ((got0, 1 - odd), (got1, odd)):
        halo_blocks(got, nblk + place * HB, w_cat, proj_ref, far_ref)
    tile_part(unroll, 3, plan_ref, proj_ref, far_ref, near_ref, cotp_ref, msg_ref, grad_ref)
    for held, place in zip((held0, held1, held2, held3), places):
        for h in range(HB):
            held[h * BLK : (h + 1) * BLK, :] = grad_ref[nblk + place * HB + h].astype(BF16)


def tiles_own_kernel(
    unroll, plan_ref, proj_ref, far_ref, near_ref, cotp_ref, msg_in, grad_in, after_ref, msg_ref, grad_ref
):
    tile_part(unroll, 0, plan_ref, proj_ref, far_ref, near_ref, cotp_ref, msg_ref, grad_ref)


def prepare_kernel(
    group_atoms,
    flip_ref,
    tiles_ref,
    count_ref,
    wave_ref,
    norm2_ref,
    w_long_ref,
    gain_ref,
    w_in_ref,
    w_out_ref,
    feats_ref,
    keep_in,
    after_ref,
    strength_ref,
    w_long_t_ref,
    w_in_t_ref,
    w_out_t_ref,
    gain_t_ref,
    feats_t_ref,
    parity_ref,
    plan_ref,
    keep_ref,
):
    parts = tile_plan(tiles_ref, count_ref, feats_ref.shape[0] // BLK)
    parts.append(jnp.full((2, plan_ref.shape[1]), flip_ref[0].astype(F32)))
    plan_ref[...] = jnp.concatenate(parts, axis=0).astype(jnp.int32)
    parity_ref[...] = jnp.full(parity_ref.shape, flip_ref[0].astype(F32))
    n = wave_ref[...].astype(F32)
    n0, n1, n2 = n[0:1], n[1:2], n[2:3]
    lead = jnp.where(n0 != 0.0, n0, jnp.where(n1 != 0.0, n1, n2))
    sign = jnp.where(lead < 0.0, -1.0, 1.0)
    n0, n1, n2 = n0 * sign, n1 * sign, n2 * sign
    pair = jnp.where(n0 == 0.0, n1 - 1.0, n0 * (2 * WMAX + 1) + n1 + (2.0 * WMAX - (2 * WMAX + 1)))
    shift = jnp.where(
        n2 == 0.0,
        0.0,
        BASE_ROWS
        + (jnp.abs(n2) - 1.0) * (2 * NPAIR)
        + jnp.where(n2 < 0.0, float(NPAIR), 0.0),
    )
    row = jnp.where((n0 == 0.0) & (n1 == 0.0), NPAIR + n2, pair + shift)
    same = lax.broadcasted_iota(jnp.int32, (HALF, row.shape[1]), 0) == row.astype(jnp.int32)
    times = jnp.sum(same.astype(F32), axis=1, keepdims=True)
    norm2 = norm2_ref[...]
    strength = times * (jnp.exp(-norm2 / 16.0) / (1.0 + norm2) * float(group_atoms) ** (-0.5))
    strength_ref[...] = jnp.broadcast_to(strength, strength_ref.shape)
    w_long_t_ref[...] = w_long_ref[...].astype(F32).T.astype(BF16)
    w_in_t_ref[...] = w_in_ref[...].astype(F32).T.astype(BF16)
    w_out_t_ref[...] = w_out_ref[...].astype(F32).T.astype(BF16)
    gain_t_ref[...] = jnp.broadcast_to(gain_ref[...], gain_t_ref.shape).T
    for b in range(feats_ref.shape[0] // BLK):
        feats_t_ref[:, b * BLK : (b + 1) * BLK] = block(feats_ref, b).astype(F32).T.astype(BF16)


def finish_kernel(
    chunk,
    lists_vmem,
    plan_vmem,
    mine_ref,
    back2,
    back3,
    back1,
    back0,
    strength_ref,
    trig_ref,
    feats_t_ref,
    msg_ref,
    w_long_t_ref,
    gain_t_ref,
    w_in_t_ref,
    w_out_t_ref,
    parity_ref,
    grad_in,
    out_hbm,
    adjoint_hbm,
    grad_ref,
    out_ref,
    lists_ref,
    plan_ref,
    sems,
):
    scalars = [
        pltpu.make_async_copy(lists_vmem, lists_ref, sems.at[1]),
        pltpu.make_async_copy(plan_vmem, plan_ref, sems.at[2]),
    ]
    for copy in scalars:
        copy.start()
    copies = []
    atoms = feats_t_ref.shape[1]
    a = strength_ref[...] * mine_ref[...].astype(F32)
    b = strength_ref[...] * back0[HB * BLK :, :].astype(F32)
    even = parity_ref[0:1, :] == 0.0
    weighted = jnp.concatenate([jnp.where(even, a, b), jnp.where(even, b, a)], axis=0).astype(BF16)
    mix_w = dot(w_long_t_ref[...], weighted, NT).astype(BF16)
    gain = jnp.concatenate([gain_t_ref[...]] * (chunk // BLK), axis=1)
    w_in_t = w_in_t_ref[...]
    w_out_t = w_out_t_ref[...]
    for step in range(atoms // chunk):
        at = slice(step * chunk, (step + 1) * chunk)
        msg = jnp.concatenate([msg_ref[step * (chunk // BLK) + i] for i in range(chunk // BLK)], axis=1)
        mixed = dot(mix_w, trig_ref[:, at]) + msg + feats_t_ref[:, at].astype(F32)
        if step == 0:
            nblk = adjoint_hbm.shape[0]
            for copy in scalars:
                copy.wait()
            odd = plan_ref[6, 0]
            for ref, direction in zip((back0, back1, back2, back3), (odd, 1 - odd, 2, 3)):
                for h in range(HB):
                    grad_ref[lists_ref[0, h, direction]] += block(ref, h).astype(F32)
            copy = pltpu.make_async_copy(grad_ref.at[pl.ds(0, nblk)], adjoint_hbm, sems.at[0])
            copy.start()
            copies.append(copy)
        scale = lax.rsqrt(jnp.mean(mixed * mixed, axis=0, keepdims=True) + 1e-06)
        normed = (mixed * scale * gain).astype(BF16)
        pre = dot(w_in_t, normed)
        half = 0.5 * pre
        hidden = (half * jnp.tanh(half) + half).astype(BF16)
        out = mixed + dot(w_out_t, hidden)
        out_ref[at, :] = out.T.astype(BF16)
        rows = pl.ds(step * chunk, chunk)
        copy = pltpu.make_async_copy(out_ref.at[rows], out_hbm.at[rows], sems.at[3 + step])
        copy.start()
        copies.append(copy)
    for copy in copies:
        copy.wait()


def call(kernel, outs, args, specs, scratch=(), us=1.0, aliases=None, out_specs=None):
    return pl.pallas_call(
        kernel,
        out_shape=outs,
        in_specs=[pl.BlockSpec(memory_space=s) for s in specs],
        out_specs=[pl.BlockSpec(memory_space=s) for s in (out_specs or (VMEM,) * len(outs))],
        scratch_shapes=list(scratch),
        input_output_aliases=aliases or {},
        compiler_params=pltpu.CompilerParams(vmem_limit_bytes=24 * 1024 * 1024),
        cost_estimate=pl.CostEstimate(
            flops=int(us * 1.1e9), bytes_accessed=int(us * 3.4e6), transcendentals=0
        ),
    )(*args)


def exchange(value, axis, partner):
    length = lax.axis_size(axis)
    return lax.ppermute(value, axis, [(i, partner(i) % length) for i in range(length)])


def body(
    feats,
    coords,
    msg_cot,
    send_list,
    tiles,
    tile_count,
    wavevec,
    w_rad_a,
    w_rad_b,
    w_charge,
    w_long,
    norm_gain,
    w_in,
    w_out,
):
    atoms, width = feats.shape
    nblk = atoms // BLK
    extent = nblk + 4 * HB
    hidden = w_in.shape[1]
    domains = lax.axis_size("dom")
    flip = (lax.axis_index("dom") % 2).astype(jnp.int32).reshape(1)
    sds = jax.ShapeDtypeStruct
    like = lambda x: sds(x.shape, x.dtype)
    unroll = 16

    near_pair = lambda i: i ^ 1
    far_pair = lambda i: i + (1 if i % 2 else -1)
    up = lambda i: i + 1
    down = lambda i: i - 1
    lists = jnp.swapaxes(send_list, 1, 2)
    tile_rows = jnp.swapaxes(tiles, 1, 2)
    tile_count = tile_count.reshape(1, 1)
    table = jnp.asarray(base_table())
    norm2 = jnp.asarray(grid_norm2())

    in_hbm = lambda x: pltpu.with_memory_space_constraint(x, pltpu.HBM)
    loads = tuple(in_hbm(x) for x in (feats, coords, msg_cot, table, w_charge))
    loaded = call(
        functools.partial(load_kernel, len(loads)),
        [like(x) for x in loads] + [sds((HB * BLK + COORD_ROWS, width), BF16)] * 4,
        (flip, in_hbm(lists), *loads),
        (SMEM,) + (pltpu.HBM,) * (1 + len(loads)),
        scratch=[SMEM(lists.shape, lists.dtype), pltpu.SemaphoreType.DMA((1 + len(loads),))],
        us=1.2,
    )
    feats, coords, msg_cot, table, w_charge = loaded[: len(loads)]
    sent = loaded[len(loads) :]
    got2 = exchange(sent[2], "group", up)
    got3 = exchange(sent[3], "group", down)
    got1 = exchange(sent[1], "dom", far_pair)

    keep, send, trig = call(
        functools.partial(struct_kernel, 256),
        [
            sds((HALF, width), F32),
            sds((HB * BLK + COORD_ROWS + HALF, width), BF16),
            sds((2 * HALF, atoms), BF16),
        ],
        (flip, feats, coords, w_charge, table, sent[0]),
        (SMEM,) + (VMEM,) * 5,
        scratch=[VMEM((2 * HALF, width), F32)],
        us=0.1,
    )
    got0 = exchange(send, "dom", near_pair)
    strength, w_long_t, w_in_t, w_out_t, gain_t, feats_t, parity, plan, keep = call(
        functools.partial(prepare_kernel, atoms * domains),
        [
            sds((HALF, width), F32),
            sds((width, width), BF16),
            sds((hidden, width), BF16),
            sds((width, hidden), BF16),
            sds((width, BLK), F32),
            sds((width, atoms), BF16),
            sds((8, width), F32),
            sds((8, tiles.shape[1]), jnp.int32),
            like(keep),
        ],
        (
            flip, tile_rows, tile_count, wavevec.T, norm2, w_long, norm_gain.reshape(1, width), w_in, w_out,
            feats, keep, send,
        ),
        (SMEM,) + (VMEM,) * 10 + (pl.ANY,),
        aliases={10: 8},
        us=0.1,
    )
    total = keep + got0[HB * BLK + COORD_ROWS :].astype(F32)
    sums = [total.astype(BF16)]
    step = 2
    while step < domains:
        total = total + exchange(sums[-1], "dom", lambda i: i ^ step).astype(F32)
        sums.append(total.astype(BF16))
        step *= 2

    proj, far, near, cotp = call(
        local_kernel,
        [
            sds((extent, width, 2 * BLK), BF16),
            sds((extent, BLK, COORD_ROWS), BF16),
            sds((nblk, COORD_ROWS, BLK), BF16),
            sds((nblk, 2 * BLK, width), BF16),
        ],
        (feats, coords, msg_cot, w_rad_a, w_rad_b, send),
        (VMEM,) * 5 + (pl.ANY,),
        us=0.1,
    )
    proj, far, msg, grad, *held = call(
        functools.partial(tiles_received_kernel, unroll),
        [like(proj), like(far), sds((nblk + 1, width, BLK), F32), sds((extent + 1, BLK, width), F32)]
        + [sds((HB * BLK, width), BF16)] * 4,
        (plan, got1, got2, got3, got0, w_rad_a, w_rad_b, near, cotp, proj, far, sums[0]),
        (VMEM,) * 11 + (pl.ANY,),
        scratch=[SMEM(plan.shape, plan.dtype), pltpu.SemaphoreType.DMA],
        us=3.0,
        aliases={9: 0, 10: 1},
    )
    msg, grad = call(
        functools.partial(tiles_own_kernel, unroll),
        [like(msg), like(grad)],
        (plan, proj, far, near, cotp, msg, grad, sums[min(1, len(sums) - 1)]),
        (SMEM,) + (VMEM,) * 6 + (pl.ANY,),
        us=5.0,
        aliases={5: 0, 6: 1},
    )
    back2 = exchange(held[2], "group", down)
    back3 = exchange(held[3], "group", up)
    back1 = exchange(held[1], "dom", far_pair)
    total = sums[-1]
    back0 = exchange(jnp.concatenate([held[0], total], axis=0), "dom", near_pair)

    chunk = atoms
    new_feats, adjoint, _ = call(
        functools.partial(finish_kernel, chunk),
        [sds((atoms, width), BF16), sds((nblk, BLK, width), F32), like(grad)],
        (
            lists, plan, total, back2, back3, back1, back0, strength, trig, feats_t, msg, w_long_t, gain_t,
            w_in_t, w_out_t, parity, grad,
        ),
        (VMEM,) * 17,
        scratch=[
            VMEM((atoms, width), BF16),
            SMEM(lists.shape, lists.dtype),
            SMEM(plan.shape, plan.dtype),
            pltpu.SemaphoreType.DMA((3 + atoms // chunk,)),
        ],
        us=3.0,
        aliases={16: 2},
        out_specs=(pltpu.HBM, pltpu.HBM, VMEM),
    )
    return (new_feats, adjoint.reshape(atoms, width))


def solution(mesh):
    split = ("group", "dom")
    return jax.shard_map(
        body,
        mesh=mesh,
        in_specs=(
            P(split, None),
            P(None, split),
            P(split, None),
            P(split, None, None),
            P(split, None, None),
            P(split),
            P(),
            P(),
            P(),
            P(),
            P(),
            P(),
            P(),
            P(),
        ),
        out_specs=(P(split, None), P(split, None)),
        check_vma=False,
    )
```

```python
import functools

import jax
import jax.numpy as jnp
import numpy as np
from jax import lax
from jax.experimental import pallas as pl
from jax.experimental.pallas import tpu as pltpu
from jax.sharding import PartitionSpec as P

BLK = 128
HB = 2
WMAX = 4
COORD_ROWS = 16

RADIAL_A = 6.0
MSG_SCALE = 1.0 / 32.0
LOG2E = 1.4426950408889634

NT = (((1,), (1,)), ((), ()))
NN = (((1,), (0,)), ((), ()))

VMEM = pltpu.VMEM
SMEM = pltpu.SMEM
BF16 = jnp.bfloat16
F32 = jnp.float32


def dot(a, b, dims=NN):
    return lax.dot_general(a, b, dims, preferred_element_type=F32)


PAIRS = [(0, b) for b in range(1, WMAX + 1)] + [
    (a, b) for a in range(1, WMAX + 1) for b in range(-WMAX, WMAX + 1)
]
NPAIR = len(PAIRS)
BASE_ROWS = 48
HALF = BASE_ROWS + WMAX * 2 * NPAIR


def base_table():
    rows = np.zeros((BASE_ROWS, COORD_ROWS), np.float32)
    for r, (a, b) in enumerate(PAIRS):
        rows[r, 0], rows[r, 1] = a, b
    for m in range(WMAX + 1):
        rows[NPAIR + m, 2] = m
    return rows


def grid_norm2():
    base = (base_table() ** 2).sum(1)
    parts = [base]
    for m in range(1, WMAX + 1):
        parts += [base[:NPAIR] + m * m] * 2
    return np.concatenate(parts).reshape(HALF, 1).astype(np.float32)


def taylor(first, count):
    coef, out = 1.0, []
    for k in range(1, first + 1):
        coef /= k
    power = first
    for _ in range(count):
        out.append(coef)
        coef = -coef / ((power + 1) * (power + 2))
        power += 2
    return out


SIN_COEF = [c * np.pi ** (2 * i + 1) for i, c in enumerate(taylor(1, 7))]
COS_COEF = [c * np.pi ** (2 * i) for i, c in enumerate(taylor(0, 8))]


def horner(z, coefs):
    acc = jnp.full_like(z, coefs[-1])
    for c in coefs[-2::-1]:
        acc = acc * z + c
    return acc


def cos_sin_turns(turns):
    r = turns - jnp.round(turns)
    z = r * r
    s = r * horner(z, SIN_COEF)
    c = horner(z, COS_COEF)
    return 1.0 - 2.0 * (s * s), 2.0 * (s * c)


def trig_chunk(table, xyz16):
    c, s = cos_sin_turns(dot(table, xyz16))
    cos_parts, sin_parts = [c.astype(BF16)], [s.astype(BF16)]
    cp, sp = c[:NPAIR], s[:NPAIR]
    for m in range(1, WMAX + 1):
        cz, sz = c[NPAIR + m : NPAIR + m + 1], s[NPAIR + m : NPAIR + m + 1]
        cc, ss, sc, cs = cp * cz, sp * sz, sp * cz, cp * sz
        cos_parts.append(jnp.concatenate([cc - ss, cc + ss], axis=0).astype(BF16))
        sin_parts.append(jnp.concatenate([sc + cs, sc - cs], axis=0).astype(BF16))
    return jnp.concatenate(cos_parts + sin_parts, axis=0)


def coords16(xyz):
    return jnp.concatenate(
        [xyz.astype(F32), jnp.zeros((COORD_ROWS - 3, xyz.shape[1]), F32)], axis=0
    ).astype(BF16)


def split3(v):
    hi = v.astype(BF16).astype(F32)
    mid = (v - hi).astype(BF16).astype(F32)
    return hi, mid, (v - hi) - mid


def dist_rows(xyz, near):
    x = xyz.astype(F32)
    hi, mid, lo = split3(jnp.sum(x * x, axis=0, keepdims=True))
    one = jnp.ones_like(hi)
    rest = jnp.zeros((COORD_ROWS - 9, x.shape[1]), F32)
    if near:
        parts = [-2.0 * x, hi, mid, lo, one, one, one, rest]
    else:
        parts = [x, one, one, one, hi, mid, lo, rest]
    return jnp.concatenate(parts, axis=0)


def block(ref, b):
    return ref[b * BLK : (b + 1) * BLK, :]


def send_block(lists_ref, direction, feats_ref, coords_ref, out_ref):
    pieces = []
    for h in range(HB):
        start = pl.multiple_of(lists_ref[0, h, direction] * BLK, BLK)
        out_ref[pl.ds(h * BLK, BLK), :] = feats_ref[pl.ds(start, BLK), :]
        pieces.append(coords_ref[:, pl.ds(start, BLK)].astype(F32))
        pieces.append(jnp.zeros((COORD_ROWS // HB - 3, BLK), F32))
    out_ref[pl.ds(HB * BLK, COORD_ROWS), :] = jnp.concatenate(pieces, axis=0).astype(BF16)


def load_kernel(n_load, flip_ref, lists_hbm, *refs):
    sources, loaded = refs[:n_load], refs[n_load : 2 * n_load]
    outs, lists_ref, sems = refs[2 * n_load : 2 * n_load + 4], refs[-2], refs[-1]
    copies = [
        pltpu.make_async_copy(src, dst, sems.at[k])
        for k, (src, dst) in enumerate(zip((lists_hbm, *sources), (lists_ref, *loaded)))
    ]
    for copy in copies:
        copy.start()
    for copy in copies[:3]:
        copy.wait()
    odd = flip_ref[0]
    for out_ref, direction in zip(outs, (odd, 1 - odd, 2, 3)):
        send_block(lists_ref, direction, loaded[0], loaded[1], out_ref)
    for copy in copies[3:]:
        copy.wait()


def struct_kernel(
    chunk, flip_ref, feats_ref, coords_ref, w_ref, table_ref, first_ref, keep_ref, send_ref, trig_ref, total_ref
):
    atoms = feats_ref.shape[0]
    table = table_ref[...].astype(BF16)
    w = w_ref[...]
    for first in range(0, atoms, chunk):
        at = slice(first, first + chunk)
        charges = dot(feats_ref[at, :], w).astype(BF16)
        trig = trig_chunk(table, coords16(coords_ref[:, at]))
        trig_ref[:, at] = trig
        part = dot(trig, charges)
        if first == 0:
            total_ref[...] = part
        else:
            total_ref[...] += part
    mine = pl.multiple_of(flip_ref[0] * HALF, 8)
    other = pl.multiple_of((1 - flip_ref[0]) * HALF, 8)
    keep_ref[...] = total_ref[pl.ds(mine, HALF), :]
    head = first_ref.shape[0]
    send_ref[0:head, :] = first_ref[...]
    send_ref[head:, :] = total_ref[pl.ds(other, HALF), :].astype(BF16)


def source_block(j, w_cat, feats, far, proj_ref, far_ref):
    both = (dot(w_cat, feats, NT) * MSG_SCALE).astype(BF16)
    proj_ref[j, :, 0:BLK] = both[:BLK]
    proj_ref[j, :, BLK:] = both[BLK:]
    far_ref[j] = far.T.astype(BF16)


def both_transposed(wa_ref, wb_ref):
    return jnp.concatenate([wa_ref[...].astype(F32).T, wb_ref[...].astype(F32).T], axis=0).astype(BF16)


def halo_blocks(got, first_block, w_cat, proj_ref, far_ref):
    tail = got[HB * BLK : HB * BLK + COORD_ROWS, :].astype(F32)
    for h in range(HB):
        at = h * (COORD_ROWS // HB)
        far = dist_rows(tail[at : at + 3], False)
        source_block(first_block + h, w_cat, block(got, h), far, proj_ref, far_ref)


def tile_plan(tiles_ref, count_ref, nblk):
    slots = tiles_ref.shape[2]
    tiles = tiles_ref[0].astype(F32)
    iota = lambda axis: lax.broadcasted_iota(jnp.int32, (slots, slots), axis)
    before = (iota(1) < iota(0)).astype(F32).astype(BF16)
    same = (iota(1) == iota(0)).astype(F32).astype(BF16)
    number = lax.broadcasted_iota(jnp.int32, (1, slots), 1)
    live = (number < count_ref[...]).astype(F32)
    own = live * (tiles[1:2] < float(nblk)).astype(F32)
    sub = lax.broadcasted_iota(jnp.int32, (8, slots), 0)
    rows = jnp.where(sub == 0, own, jnp.where(sub == 1, live - own, 0.0)).astype(BF16)
    columns = dot(jnp.concatenate([before, same], axis=0), rows, NT)
    counts = dot(rows, jnp.ones((slots, slots), BF16))
    both = jnp.where(sub % 2 == 0, tiles[0:1], tiles[1:2]).astype(BF16)
    parts = []
    for k in range(2):
        place = columns[:slots, k : k + 1].astype(jnp.int32)
        here = columns[slots:, k : k + 1] > 0.5
        moved = dot(both, ((iota(1) == place) & here).astype(F32).astype(BF16))
        parts += [moved[0:2], counts[k : k + 1]]
    return parts


def local_kernel(
    feats_ref,
    coords_ref,
    cot_ref,
    wa_ref,
    wb_ref,
    after_ref,
    proj_ref,
    far_ref,
    near_ref,
    cotp_ref,
):
    nblk = feats_ref.shape[0] // BLK
    w_cat = both_transposed(wa_ref, wb_ref)
    w_side = jnp.concatenate([wa_ref[...], wb_ref[...]], axis=0)
    near = dist_rows(coords_ref[...], True).astype(BF16)
    far = dist_rows(coords_ref[...], False)
    for b in range(nblk):
        at = slice(b * BLK, (b + 1) * BLK)
        source_block(b, w_cat, block(feats_ref, b), far[:, at], proj_ref, far_ref)
        near_ref[b] = near[:, at]
        both = (dot(block(cot_ref, b), w_side, NT) * MSG_SCALE).astype(BF16)
        cotp_ref[b, 0:BLK, :] = both[:, :BLK]
        cotp_ref[b, BLK:, :] = both[:, BLK:]


def tile_part(unroll, row, plan_ref, proj_ref, far_ref, near_ref, cotp_ref, msg_ref, grad_ref):
    spare_i, spare_j = msg_ref.shape[0] - 1, grad_ref.shape[0] - 1
    slots = plan_ref.shape[1]
    count = plan_ref[row + 2, 0]

    def group(first, width):
        idx = []
        for u in range(width):
            t = first + u
            at = jnp.minimum(t, slots - 1)
            i, j, live = plan_ref[row, at], plan_ref[row + 1, at], t < count
            idx.append((i, j, jnp.where(live, i, spare_i), jnp.where(live, j, spare_j)))
        kers = []
        for i, j, _, _ in idx:
            d = dot(far_ref[j], near_ref[i])
            a = jnp.exp2(d * (-RADIAL_A * LOG2E))
            a2 = a * a
            b = (a2 * a2) * a
            kers.append((a.astype(BF16), b.astype(BF16)))
        for (i, j, to_i, to_j), (ka, kb) in zip(idx, kers):
            msg_ref[to_i] += dot(proj_ref[j], jnp.concatenate([ka, kb], axis=0))
            grad_ref[to_j] += dot(jnp.concatenate([ka, kb], axis=1), cotp_ref[i])

    half = unroll // 2
    whole = (count + half - 1) // unroll

    @pl.loop(0, whole)
    def _(step):
        group(step * unroll, unroll)

    @pl.when(count > whole * unroll)
    def _():
        group(whole * unroll, half)


def tiles_received_kernel(
    unroll,
    plan_vmem,
    got1,
    got2,
    got3,
    got0,
    wa_ref,
    wb_ref,
    near_ref,
    cotp_ref,
    proj_in,
    far_in,
    after_ref,
    proj_ref,
    far_ref,
    msg_ref,
    grad_ref,
    held0,
    held1,
    held2,
    held3,
    plan_ref,
    sem,
):
    copy = pltpu.make_async_copy(plan_vmem, plan_ref, sem)
    copy.start()
    nblk = near_ref.shape[0]
    w_cat = both_transposed(wa_ref, wb_ref)
    for got, place in ((got2, 2), (got3, 3)):
        halo_blocks(got, nblk + place * HB, w_cat, proj_ref, far_ref)
    msg_ref[...] = jnp.zeros_like(msg_ref)
    grad_ref[...] = jnp.zeros_like(grad_ref)
    copy.wait()
    odd = plan_ref[6, 0]
    places = (1 - odd, odd, 2, 3)
    for got, place in ((got0, 1 - odd), (got1, odd)):
        halo_blocks(got, nblk + place * HB, w_cat, proj_ref, far_ref)
    tile_part(unroll, 3, plan_ref, proj_ref, far_ref, near_ref, cotp_ref, msg_ref, grad_ref)
    for held, place in zip((held0, held1, held2, held3), places):
        for h in range(HB):
            held[h * BLK : (h + 1) * BLK, :] = grad_ref[nblk + place * HB + h].astype(BF16)


def tiles_own_kernel(
    unroll, plan_ref, proj_ref, far_ref, near_ref, cotp_ref, msg_in, grad_in, after_ref, msg_ref, grad_ref
):
    tile_part(unroll, 0, plan_ref, proj_ref, far_ref, near_ref, cotp_ref, msg_ref, grad_ref)


def prepare_kernel(
    group_atoms,
    flip_ref,
    tiles_ref,
    count_ref,
    wave_ref,
    norm2_ref,
    w_long_ref,
    gain_ref,
    w_in_ref,
    w_out_ref,
    feats_ref,
    keep_in,
    after_ref,
    strength_ref,
    w_long_t_ref,
    w_in_t_ref,
    w_out_t_ref,
    gain_t_ref,
    feats_t_ref,
    parity_ref,
    plan_ref,
    keep_ref,
):
    parts = tile_plan(tiles_ref, count_ref, feats_ref.shape[0] // BLK)
    parts.append(jnp.full((2, plan_ref.shape[1]), flip_ref[0].astype(F32)))
    plan_ref[...] = jnp.concatenate(parts, axis=0).astype(jnp.int32)
    parity_ref[...] = jnp.full(parity_ref.shape, flip_ref[0].astype(F32))
    n = wave_ref[...].astype(F32)
    n0, n1, n2 = n[0:1], n[1:2], n[2:3]
    lead = jnp.where(n0 != 0.0, n0, jnp.where(n1 != 0.0, n1, n2))
    sign = jnp.where(lead < 0.0, -1.0, 1.0)
    n0, n1, n2 = n0 * sign, n1 * sign, n2 * sign
    pair = jnp.where(n0 == 0.0, n1 - 1.0, n0 * (2 * WMAX + 1) + n1 + (2.0 * WMAX - (2 * WMAX + 1)))
    shift = jnp.where(
        n2 == 0.0,
        0.0,
        BASE_ROWS
        + (jnp.abs(n2) - 1.0) * (2 * NPAIR)
        + jnp.where(n2 < 0.0, float(NPAIR), 0.0),
    )
    row = jnp.where((n0 == 0.0) & (n1 == 0.0), NPAIR + n2, pair + shift)
    same = lax.broadcasted_iota(jnp.int32, (HALF, row.shape[1]), 0) == row.astype(jnp.int32)
    times = jnp.sum(same.astype(F32), axis=1, keepdims=True)
    norm2 = norm2_ref[...]
    strength = times * (jnp.exp(-norm2 / 16.0) / (1.0 + norm2) * float(group_atoms) ** (-0.5))
    strength_ref[...] = jnp.broadcast_to(strength, strength_ref.shape)
    w_long_t_ref[...] = w_long_ref[...].astype(F32).T.astype(BF16)
    w_in_t_ref[...] = w_in_ref[...].astype(F32).T.astype(BF16)
    w_out_t_ref[...] = w_out_ref[...].astype(F32).T.astype(BF16)
    gain_t_ref[...] = jnp.broadcast_to(gain_ref[...], gain_t_ref.shape).T
    for b in range(feats_ref.shape[0] // BLK):
        feats_t_ref[:, b * BLK : (b + 1) * BLK] = block(feats_ref, b).astype(F32).T.astype(BF16)


def finish_kernel(
    chunk,
    lists_vmem,
    plan_vmem,
    mine_ref,
    back2,
    back3,
    back1,
    back0,
    strength_ref,
    trig_ref,
    feats_t_ref,
    msg_ref,
    w_long_t_ref,
    gain_t_ref,
    w_in_t_ref,
    w_out_t_ref,
    parity_ref,
    grad_in,
    out_hbm,
    adjoint_hbm,
    grad_ref,
    out_ref,
    lists_ref,
    plan_ref,
    sems,
):
    scalars = [
        pltpu.make_async_copy(lists_vmem, lists_ref, sems.at[1]),
        pltpu.make_async_copy(plan_vmem, plan_ref, sems.at[2]),
    ]
    for copy in scalars:
        copy.start()
    copies = []
    atoms = feats_t_ref.shape[1]
    a = strength_ref[...] * mine_ref[...].astype(F32)
    b = strength_ref[...] * back0[HB * BLK :, :].astype(F32)
    even = parity_ref[0:1, :] == 0.0
    weighted = jnp.concatenate([jnp.where(even, a, b), jnp.where(even, b, a)], axis=0).astype(BF16)
    mix_w = dot(w_long_t_ref[...], weighted, NT).astype(BF16)
    gain = jnp.concatenate([gain_t_ref[...]] * (chunk // BLK), axis=1)
    w_in_t = w_in_t_ref[...]
    w_out_t = w_out_t_ref[...]
    for step in range(atoms // chunk):
        at = slice(step * chunk, (step + 1) * chunk)
        msg = jnp.concatenate([msg_ref[step * (chunk // BLK) + i] for i in range(chunk // BLK)], axis=1)
        mixed = dot(mix_w, trig_ref[:, at]) + msg + feats_t_ref[:, at].astype(F32)
        if step == 0:
            nblk = adjoint_hbm.shape[0]
            for copy in scalars:
                copy.wait()
            odd = plan_ref[6, 0]
            for ref, direction in zip((back0, back1, back2, back3), (odd, 1 - odd, 2, 3)):
                for h in range(HB):
                    grad_ref[lists_ref[0, h, direction]] += block(ref, h).astype(F32)
            copy = pltpu.make_async_copy(grad_ref.at[pl.ds(0, nblk)], adjoint_hbm, sems.at[0])
            copy.start()
            copies.append(copy)
        scale = lax.rsqrt(jnp.mean(mixed * mixed, axis=0, keepdims=True) + 1e-06)
        normed = (mixed * scale * gain).astype(BF16)
        pre = dot(w_in_t, normed)
        half = 0.5 * pre
        hidden = (half * jnp.tanh(half) + half).astype(BF16)
        out = mixed + dot(w_out_t, hidden)
        out_ref[at, :] = out.T.astype(BF16)
        rows = pl.ds(step * chunk, chunk)
        copy = pltpu.make_async_copy(out_ref.at[rows], out_hbm.at[rows], sems.at[3 + step])
        copy.start()
        copies.append(copy)
    for copy in copies:
        copy.wait()


def call(kernel, outs, args, specs, scratch=(), us=1.0, aliases=None, out_specs=None):
    return pl.pallas_call(
        kernel,
        out_shape=outs,
        in_specs=[pl.BlockSpec(memory_space=s) for s in specs],
        out_specs=[pl.BlockSpec(memory_space=s) for s in (out_specs or (VMEM,) * len(outs))],
        scratch_shapes=list(scratch),
        input_output_aliases=aliases or {},
        compiler_params=pltpu.CompilerParams(vmem_limit_bytes=24 * 1024 * 1024),
        cost_estimate=pl.CostEstimate(
            flops=int(us * 1.1e9), bytes_accessed=int(us * 3.4e6), transcendentals=0
        ),
    )(*args)


def exchange(value, axis, partner):
    length = lax.axis_size(axis)
    return lax.ppermute(value, axis, [(i, partner(i) % length) for i in range(length)])


def body(
    feats,
    coords,
    msg_cot,
    send_list,
    tiles,
    tile_count,
    wavevec,
    w_rad_a,
    w_rad_b,
    w_charge,
    w_long,
    norm_gain,
    w_in,
    w_out,
):
    atoms, width = feats.shape
    nblk = atoms // BLK
    extent = nblk + 4 * HB
    hidden = w_in.shape[1]
    domains = lax.axis_size("dom")
    flip = (lax.axis_index("dom") % 2).astype(jnp.int32).reshape(1)
    sds = jax.ShapeDtypeStruct
    like = lambda x: sds(x.shape, x.dtype)
    unroll = 16

    near_pair = lambda i: i ^ 1
    far_pair = lambda i: i + (1 if i % 2 else -1)
    up = lambda i: i + 1
    down = lambda i: i - 1
    lists = jnp.swapaxes(send_list, 1, 2)
    tile_rows = jnp.swapaxes(tiles, 1, 2)
    tile_count = tile_count.reshape(1, 1)
    table = jnp.asarray(base_table())
    norm2 = jnp.asarray(grid_norm2())

    in_hbm = lambda x: pltpu.with_memory_space_constraint(x, pltpu.HBM)
    loads = tuple(in_hbm(x) for x in (feats, coords, msg_cot, table, w_charge))
    loaded = call(
        functools.partial(load_kernel, len(loads)),
        [like(x) for x in loads] + [sds((HB * BLK + COORD_ROWS, width), BF16)] * 4,
        (flip, in_hbm(lists), *loads),
        (SMEM,) + (pltpu.HBM,) * (1 + len(loads)),
        scratch=[SMEM(lists.shape, lists.dtype), pltpu.SemaphoreType.DMA((1 + len(loads),))],
        us=1.2,
    )
    feats, coords, msg_cot, table, w_charge = loaded[: len(loads)]
    sent = loaded[len(loads) :]
    got2 = exchange(sent[2], "group", up)
    got3 = exchange(sent[3], "group", down)
    got1 = exchange(sent[1], "dom", far_pair)

    keep, send, trig = call(
        functools.partial(struct_kernel, min(atoms, 1024)),
        [
            sds((HALF, width), F32),
            sds((HB * BLK + COORD_ROWS + HALF, width), BF16),
            sds((2 * HALF, atoms), BF16),
        ],
        (flip, feats, coords, w_charge, table, sent[0]),
        (SMEM,) + (VMEM,) * 5,
        scratch=[VMEM((2 * HALF, width), F32)],
        us=0.1,
    )
    got0 = exchange(send, "dom", near_pair)
    strength, w_long_t, w_in_t, w_out_t, gain_t, feats_t, parity, plan, keep = call(
        functools.partial(prepare_kernel, atoms * domains),
        [
            sds((HALF, width), F32),
            sds((width, width), BF16),
            sds((hidden, width), BF16),
            sds((width, hidden), BF16),
            sds((width, BLK), F32),
            sds((width, atoms), BF16),
            sds((8, width), F32),
            sds((8, tiles.shape[1]), jnp.int32),
            like(keep),
        ],
        (
            flip, tile_rows, tile_count, wavevec.T, norm2, w_long, norm_gain.reshape(1, width), w_in, w_out,
            feats, keep, send,
        ),
        (SMEM,) + (VMEM,) * 10 + (pl.ANY,),
        aliases={10: 8},
        us=0.1,
    )
    total = keep + got0[HB * BLK + COORD_ROWS :].astype(F32)
    sums = [total.astype(BF16)]
    step = 2
    while step < domains:
        total = total + exchange(sums[-1], "dom", lambda i: i ^ step).astype(F32)
        sums.append(total.astype(BF16))
        step *= 2

    proj, far, near, cotp = call(
        local_kernel,
        [
            sds((extent, width, 2 * BLK), BF16),
            sds((extent, BLK, COORD_ROWS), BF16),
            sds((nblk, COORD_ROWS, BLK), BF16),
            sds((nblk, 2 * BLK, width), BF16),
        ],
        (feats, coords, msg_cot, w_rad_a, w_rad_b, send),
        (VMEM,) * 5 + (pl.ANY,),
        us=0.1,
    )
    proj, far, msg, grad, *held = call(
        functools.partial(tiles_received_kernel, unroll),
        [like(proj), like(far), sds((nblk + 1, width, BLK), F32), sds((extent + 1, BLK, width), F32)]
        + [sds((HB * BLK, width), BF16)] * 4,
        (plan, got1, got2, got3, got0, w_rad_a, w_rad_b, near, cotp, proj, far, sums[0]),
        (VMEM,) * 11 + (pl.ANY,),
        scratch=[SMEM(plan.shape, plan.dtype), pltpu.SemaphoreType.DMA],
        us=3.0,
        aliases={9: 0, 10: 1},
    )
    msg, grad = call(
        functools.partial(tiles_own_kernel, unroll),
        [like(msg), like(grad)],
        (plan, proj, far, near, cotp, msg, grad, sums[min(1, len(sums) - 1)]),
        (SMEM,) + (VMEM,) * 6 + (pl.ANY,),
        us=5.0,
        aliases={5: 0, 6: 1},
    )
    back2 = exchange(held[2], "group", down)
    back3 = exchange(held[3], "group", up)
    back1 = exchange(held[1], "dom", far_pair)
    total = sums[-1]
    back0 = exchange(jnp.concatenate([held[0], total], axis=0), "dom", near_pair)

    chunk = atoms
    new_feats, adjoint, _ = call(
        functools.partial(finish_kernel, chunk),
        [sds((atoms, width), BF16), sds((nblk, BLK, width), F32), like(grad)],
        (
            lists, plan, total, back2, back3, back1, back0, strength, trig, feats_t, msg, w_long_t, gain_t,
            w_in_t, w_out_t, parity, grad,
        ),
        (VMEM,) * 17,
        scratch=[
            VMEM((atoms, width), BF16),
            SMEM(lists.shape, lists.dtype),
            SMEM(plan.shape, plan.dtype),
            pltpu.SemaphoreType.DMA((3 + atoms // chunk,)),
        ],
        us=3.0,
        aliases={16: 2},
        out_specs=(pltpu.HBM, pltpu.HBM, VMEM),
    )
    return (new_feats, adjoint.reshape(atoms, width))


def solution(mesh):
    split = ("group", "dom")
    return jax.shard_map(
        body,
        mesh=mesh,
        in_specs=(
            P(split, None),
            P(None, split),
            P(split, None),
            P(split, None, None),
            P(split, None, None),
            P(split),
            P(),
            P(),
            P(),
            P(),
            P(),
            P(),
            P(),
            P(),
        ),
        out_specs=(P(split, None), P(split, None)),
        check_vma=False,
    )
```
